128 devices in a mesh: ctx: 8 (over y_lo, x), exp: 16 (over z, y_hi, core).
Axes of the slice: x: 4, y: 4 (y_hi: 2, y_lo: 2; y = y_hi * 2 + y_lo), z: 4, core: 2. Of those that a mesh axis runs over, the one named last changes fastest.
Arguments:
- resid_in: bfloat16 [16384, 2880], P(('exp', 'ctx')), may hold values from -6 to 6
- queries: bfloat16 [16384, 4096], P(('exp', 'ctx')), may hold values from -6 to 6
- keys: bfloat16 [16384, 512], P(('exp', 'ctx')), may hold values from -6 to 6
- values: bfloat16 [16384, 512], P(('exp', 'ctx')), may hold values from -6 to 6
- sinks: float32 [64], replicated, may hold values from 2 to 7
- segments: int32 [16384], P(('exp', 'ctx')), may hold values from 0 to 31, never falling along the last dimension, each value on 1 to 1024 neighbouring positions
- norm_gain: float32 [2880], replicated, may hold values from 0.1 to 1.9
- out_weight: bfloat16 [4096, 2880], P('ctx'), may hold values from -0.75 to 0.75
- gate_weight: bfloat16 [16, 2880, 2880], P('exp', None, 'ctx'), may hold values from -0.109375 to 0.109375
- up_weight: bfloat16 [16, 2880, 2880], P('exp', None, 'ctx'), may hold values from -0.109375 to 0.109375
- down_weight: bfloat16 [16, 2880, 2880], P('exp', 'ctx'), may hold values from -0.109375 to 0.109375
- expert_ids: int32 [16384, 4], P(('exp', 'ctx')), may hold values from 0 to 127, as said below
- route_weights: float32 [16384, 4], P(('exp', 'ctx')), may hold values from 0.1 to 1
Outputs:
- resid_out: bfloat16 [16384, 2880], P(('exp', 'ctx'))
The draws below stay inside these ranges and needn't reach their ends.
Inputs may be any that keep to these rules, and one draw needn't show every extreme that they name: `expert_ids`: column k of a row names an expert in [k * 32, (k + 1) * 32). Within the rows of one device (aligned blocks of 128 rows) no evaluated expert is named more than 8 times, and one evaluated expert is named exactly 8 times in every block.
All inputs are finite; a program needn't handle non-finite values.
Results may differ from the reference program's by a relative error of at most 0.018.
Values may be sent and summed in bfloat16 or wider, within the bound.
No kernel may reach another device: no remote copies, remote signals or barrier semaphores. Data moves between devices by JAX's collectives and lax.ppermute only.
A program may use at most 128 MiB of HBM per device.

```python
import math
import jax
import jax.numpy as jnp
import numpy as np
from jax import lax

D = 2880
QUERY_HEADS = 64
KEY_VALUE_HEADS = 8
HEAD_SIZE = 64
FF = 2880
ALL_EXPERTS = 128
TOPK = 4
TOK_DEV = 128
CAP = 8
EXPERTS = 16
SEQUENCE_LENGTH = 1024
TOKEN_COUNT = 16384
N_EXP = 16


def draw_queries(key, part):
    key = jax.random.fold_in(key, 3)
    score_field = jnp.clip(jax.random.normal(key, (TOKEN_COUNT, QUERY_HEADS * HEAD_SIZE), jnp.float32), -6.0, 6.0)
    return score_field.astype(jnp.bfloat16)


def draw_keys(key, part):
    key = jax.random.fold_in(key, 4)
    score_field = jnp.clip(jax.random.normal(key, (TOKEN_COUNT, KEY_VALUE_HEADS * HEAD_SIZE), jnp.float32), -6.0, 6.0)
    return score_field.astype(jnp.bfloat16)


def draw_expert_ids(key, part):
    key = jax.random.fold_in(key, 5)
    leading_index, second, third = jax.random.split(key, 3)
    blocks = TOKEN_COUNT // TOK_DEV
    quarter = ALL_EXPERTS // TOPK
    window = EXPERTS // TOPK
    local = jax.random.randint(leading_index, (blocks, TOK_DEV, TOPK), 0, quarter)
    hot = jax.random.randint(second, (), 0, window)
    block_keys = jax.random.split(third, blocks)
    order = jax.vmap(lambda one: jax.random.permutation(one, TOK_DEV))(block_keys)
    forced = order < CAP
    lead = local[:, :, 0]
    lead = jnp.where(forced, hot, jnp.where(lead == hot, hot + window, lead))
    local = local.at[:, :, 0].set(lead)
    onehot = (local[..., None] == jnp.arange(window)).astype(jnp.int32)
    before = jnp.cumsum(onehot, axis=1) - onehot
    own_rank = jnp.sum(onehot * before, axis=-1)
    over = (local < window) & (own_rank >= CAP)
    local = jnp.where(over, local + window, local)
    chosen = local + jnp.arange(TOPK) * quarter
    return chosen.reshape(TOKEN_COUNT, TOPK).astype(jnp.int32)


def shard_levels(key, dims, shards, smallest, top_value):
    def one(position, blocks):
        heights = jax.random.uniform(jax.random.fold_in(jax.random.fold_in(key, 6), position), (blocks,), jnp.float32, smallest / len(shards), top_value / len(shards))
        return jnp.repeat(jnp.exp(heights), dims[position] // blocks).reshape((-1,) + (1,) * (len(dims) - position - 1))

    factor_of = one(*shards[0])
    for cut in shards[1:]:
        factor_of = factor_of * one(*cut)
    return factor_of


def split_up(amount, total, bound, skew):
    portions = [(1 << 20) // math.isqrt(rank ** skew) + 1 for rank in range(2, amount + 1)]
    surplus, counts = total - bound - (amount - 1), [1] * (amount - 1)
    while surplus > 0:
        free = [i for i in range(amount - 1) if counts[i] < bound]
        pool, remaining = sum([portions[i] for i in free]), surplus
        for i in free:
            more = min(bound - counts[i], max(1, remaining * portions[i] // pool), surplus)
            counts[i] = counts[i] + more
            surplus = surplus - more
    return np.array([bound] + counts)


def uneven_parts(own_key, amount, total, reach, skew):
    if amount == 2:
        one = jax.random.randint(own_key, (), max(1, total - reach), min(reach, total - 1) + 1)
        return jnp.stack([one, total - one])
    lengths = jnp.asarray(split_up(amount, total, reach, skew), jnp.int32)
    couples = (amount - 1) // 2
    donor, sink = lengths[1:1 + 2 * couples:2], lengths[2:2 + 2 * couples:2]
    slack = jnp.minimum(donor - 1, reach - sink)
    passed = jax.random.randint(jax.random.fold_in(own_key, 1), (couples,), 0, 1 << 20) % (slack + 1)
    lengths = lengths.at[1:1 + 2 * couples:2].set(donor - passed).at[2:2 + 2 * couples:2].set(sink + passed)
    return lengths[jax.random.permutation(jax.random.fold_in(own_key, 2), amount)]


def centred(stream_key, shape, spread, bound, cuts=(), kind=jnp.bfloat16):
    values = spread * jax.random.normal(stream_key, shape, jnp.float32)
    if cuts:
        values = values * shard_levels(stream_key, shape, cuts, -0.22, 0.18)
    return jnp.clip(values, -bound, bound).astype(kind)


def setup_inputs(seed: int = 0) -> dict:
    key_list = jax.random.split(jax.random.key(seed), 14)
    return {
        "resid_in": centred(key_list[0], (TOKEN_COUNT, D), 1.0, 6.0, ((0, 128),)),
        "queries": draw_queries(jax.random.fold_in(key_list[13], 71), 0),
        "keys": draw_keys(jax.random.fold_in(key_list[13], 71), 0),
        "values": centred(key_list[3], (TOKEN_COUNT, KEY_VALUE_HEADS * HEAD_SIZE), 1.0, 6.0, ((0, 128),)),
        "sinks": jnp.clip(jax.random.uniform(key_list[4], (QUERY_HEADS,), jnp.float32, 2.0, 7.0), 2.0, 7.0),
        "segments": jnp.searchsorted(jnp.cumsum(uneven_parts(key_list[5], 2 * N_EXP, TOKEN_COUNT, SEQUENCE_LENGTH, 2)), jnp.arange(TOKEN_COUNT), side="right").astype(jnp.int32),
        "norm_gain": jnp.clip(1.0 + 0.18 * jax.random.normal(key_list[6], (D,), jnp.float32), 0.1, 1.9),
        "out_weight": centred(key_list[7], (QUERY_HEADS * HEAD_SIZE, D), HEAD_SIZE ** -0.5, 0.75, ((0, 8),)),
        "gate_weight": centred(key_list[8], (EXPERTS, D, FF), D ** -0.5, 0.109375, ((0, 16), (2, 8))),
        "up_weight": centred(key_list[9], (EXPERTS, D, FF), D ** -0.5, 0.109375, ((0, 16), (2, 8))),
        "down_weight": centred(key_list[10], (EXPERTS, FF, D), FF ** -0.5, 0.109375, ((0, 16), (1, 8))),
        "expert_ids": draw_expert_ids(jax.random.fold_in(key_list[13], 71), 0),
        "route_weights": jnp.clip(jnp.exp(math.log(1.0) - 2.3025851 * jax.random.uniform(key_list[12], (TOKEN_COUNT, TOPK), jnp.float32) ** shard_levels(key_list[12], (TOKEN_COUNT, TOPK), ((0, 128),), -0.2, 0.2)), 0.1, 1.0),
    }


def attend_group(args):
    query_rows, key_rows, value_rows, sink_row, sequence_documents = args
    places = jnp.arange(SEQUENCE_LENGTH)
    scores = jnp.einsum('tjd,kd->tjk', query_rows.astype(jnp.float32), key_rows.astype(jnp.float32)) * 0.125
    allowed = (places[None, :] <= places[:, None]) & (sequence_documents[:, None] == sequence_documents[None, :])
    scores = jnp.where(allowed[:, None, :], scores, -jnp.inf)
    top_choice = jnp.maximum(lax.optimization_barrier(jnp.max(scores, axis=-1)), sink_row[None, :])
    prob = jnp.exp(scores - top_choice[..., None])
    softmax_divisor = lax.optimization_barrier(jnp.sum(prob, axis=-1)) + jnp.exp(sink_row[None, :] - top_choice)
    rounded = lax.optimization_barrier(prob.astype(jnp.bfloat16)).astype(jnp.float32)
    summed = jnp.einsum('tjk,kd->tjd', rounded, value_rows.astype(jnp.float32))
    return summed / softmax_divisor[..., None]

def attend_sequence(args):
    sequence_queries, sequence_keys, sequence_values, sequence_documents, sink_logits = args
    document_labels = jnp.broadcast_to(sequence_documents[None, :], (KEY_VALUE_HEADS, SEQUENCE_LENGTH))
    outs = lax.map(attend_group, (sequence_queries.transpose(1, 0, 2, 3), sequence_keys.transpose(1, 0, 2), sequence_values.transpose(1, 0, 2), sink_logits, document_labels))
    return outs.transpose(1, 0, 2, 3)

def reference(resid_in, queries, keys, values, sinks, segments, norm_gain, out_weight, gate_weight, up_weight, down_weight, expert_ids, route_weights):
    query_group = QUERY_HEADS // KEY_VALUE_HEADS
    n_ctx = SEQUENCE_LENGTH // TOK_DEV
    sequence_queries = queries.reshape(N_EXP, SEQUENCE_LENGTH, KEY_VALUE_HEADS, query_group, HEAD_SIZE)
    sequence_keys = keys.reshape(N_EXP, SEQUENCE_LENGTH, KEY_VALUE_HEADS, HEAD_SIZE)
    sequence_values = values.reshape(N_EXP, SEQUENCE_LENGTH, KEY_VALUE_HEADS, HEAD_SIZE)
    sequence_documents = segments.reshape(N_EXP, SEQUENCE_LENGTH)
    sink_logits = jnp.broadcast_to(sinks.reshape(1, KEY_VALUE_HEADS, query_group), (N_EXP, KEY_VALUE_HEADS, query_group))
    attn = lax.map(attend_sequence, (sequence_queries, sequence_keys, sequence_values, sequence_documents, sink_logits))
    attn = attn.reshape(TOKEN_COUNT, QUERY_HEADS * HEAD_SIZE).astype(jnp.bfloat16)
    width = QUERY_HEADS // n_ctx * HEAD_SIZE

    def add_heads(index, total):
        piece = lax.dynamic_slice_in_dim(attn, index * width, width, 1)
        rows_w = lax.dynamic_slice_in_dim(out_weight, index * width, width, 0)
        part = jnp.dot(piece, rows_w, preferred_element_type=jnp.float32)
        return total + lax.optimization_barrier(part.astype(jnp.bfloat16)).astype(jnp.float32)
    proj = lax.fori_loop(0, n_ctx, add_heads, jnp.zeros((TOKEN_COUNT, D), jnp.float32))
    hidden = resid_in.astype(jnp.float32) + proj
    scale = lax.rsqrt(lax.optimization_barrier(jnp.mean(hidden * hidden, axis=-1, keepdims=True)) + 1e-05)
    normed = (hidden * scale * norm_gain[None, :]).astype(jnp.bfloat16)
    quarter = ALL_EXPERTS // TOPK
    window = N_EXP // TOPK
    local = expert_ids % quarter
    valid = local < window
    chosen = jnp.where(valid, expert_ids // quarter * window + local, -1).reshape(-1)
    rows_cap = TOKEN_COUNT // TOK_DEV * CAP
    hid_group = FF // n_ctx

    def one_expert(index):
        hits = chosen == index
        pairs = jnp.nonzero(hits, size=rows_cap, fill_value=0)[0].astype(jnp.int32)
        live = jnp.arange(rows_cap) < jnp.sum(hits.astype(jnp.int32))
        rows_x = normed[pairs // TOPK]
        gate = jnp.dot(rows_x, gate_weight[index], preferred_element_type=jnp.float32)
        upper = jnp.dot(rows_x, up_weight[index], preferred_element_type=jnp.float32)
        act = ((upper + 1.0) * gate * jax.nn.sigmoid(1.702 * gate)).astype(jnp.bfloat16)
        down_here = down_weight[index]

        def add_units(block, total):
            piece = lax.dynamic_slice_in_dim(act, block * hid_group, hid_group, 1)
            rows_w = lax.dynamic_slice_in_dim(down_here, block * hid_group, hid_group, 0)
            part = jnp.dot(piece, rows_w, preferred_element_type=jnp.float32)
            return total + lax.optimization_barrier(part.astype(jnp.bfloat16)).astype(jnp.float32)
        result = lax.fori_loop(0, n_ctx, add_units, jnp.zeros((rows_cap, D), jnp.float32)).astype(jnp.bfloat16)
        return (pairs, jnp.where(live[:, None], result, jnp.zeros_like(result)))
    pairs, outputs = lax.map(one_expert, jnp.arange(N_EXP))
    weights_flat = route_weights.reshape(-1)
    contrib = outputs.astype(jnp.float32) * weights_flat[pairs][..., None]
    moe = jnp.zeros((TOKEN_COUNT, D), jnp.float32).at[(pairs // TOPK).reshape(-1)].add(contrib.reshape(-1, D))
    return (hidden + moe).astype(jnp.bfloat16)
```

```python
import functools

import jax
import jax.numpy as jnp
from jax import lax
from jax.experimental import pallas as pl
from jax.experimental.pallas import tpu as pltpu
from jax.sharding import PartitionSpec as P

D = 2880
QUERY_HEADS = 64
KEY_VALUE_HEADS = 8
HEAD_SIZE = 64
ALL_EXPERTS = 128
TOPK = 4
CAP = 8
TOK = 128
FFS = 360
NX = 4
QUARTER = ALL_EXPERTS // TOPK
WINDOW = 4
DOC_ROWS = 16
PACK_ROWS = TOK + DOC_ROWS
PACK_COLS = 1280
HALF = D // 2
MIB = 1024 * 1024

VMEM = pltpu.VMEM
ANY = pl.ANY
SMEM = pltpu.SMEM

RIGHT = [(4 * y + x, 4 * y + (x + 1) % 4) for y in range(2) for x in range(4)]
LEFT = [(4 * y + x, 4 * y + (x + 3) % 4) for y in range(2) for x in range(4)]
FLIP = [(c, c ^ 4) for c in range(8)]

NT = (((1,), (1,)), ((), ()))
TN = (((0,), (0,)), ((), ()))


def go_right(v):
    return lax.ppermute(v, "ctx", RIGHT)


def go_left(v):
    return lax.ppermute(v, "ctx", LEFT)


def go_flip(v):
    return lax.ppermute(v, "ctx", FLIP)


def params(mib):
    return pltpu.CompilerParams(vmem_limit_bytes=mib * MIB)


def spec(space):
    return pl.BlockSpec(memory_space=space)


def add(*pieces):
    total = pieces[0].astype(jnp.float32)
    for piece in pieces[1:]:
        total = total + piece.astype(jnp.float32)
    return total.astype(jnp.bfloat16)


def pack_kernel(q_ref, k_ref, v_ref, seg_ref, out_ref):
    lane = lax.broadcasted_iota(jnp.int32, (TOK, 128), 1)
    docs = jnp.broadcast_to(seg_ref[...].astype(jnp.float32), (DOC_ROWS, 128))
    eighth = jnp.asarray(0.125, jnp.bfloat16)
    for x in range(NX):
        out_ref[x, :TOK, 0:512] = q_ref[:, 512 * x : 512 * x + 512] * eighth
        out_ref[x, :TOK, 512:1024] = q_ref[:, 2048 + 512 * x : 2048 + 512 * x + 512] * eighth
        for ref, start in ((k_ref, 1024), (v_ref, 1152)):
            base = 128 * (x // 2)
            low = ref[:, base : base + 128].astype(jnp.float32)
            high = ref[:, 256 + base : 256 + base + 128].astype(jnp.float32)
            if x % 2 == 0:
                high = pltpu.roll(high, 64, 1)
            else:
                low = pltpu.roll(low, 64, 1)
            out_ref[x, :TOK, start : start + 128] = jnp.where(lane < 64, low, high).astype(
                jnp.bfloat16
            )
        out_ref[x, TOK:, 0:1024] = jnp.zeros((DOC_ROWS, 1024), jnp.bfloat16)
        out_ref[x, TOK:, 1024:1152] = docs.astype(jnp.bfloat16)
        out_ref[x, TOK:, 1152:1280] = jnp.zeros((DOC_ROWS, 128), jnp.bfloat16)


def pack(queries, keys, values, segments):
    return pl.pallas_call(
        pack_kernel,
        out_shape=jax.ShapeDtypeStruct((NX, PACK_ROWS, PACK_COLS), jnp.bfloat16),
        in_specs=[spec(VMEM)] * 4,
        out_specs=spec(VMEM),
        compiler_params=params(12),
        cost_estimate=pl.CostEstimate(flops=0, bytes_accessed=5 << 20, transcendentals=0),
    )(queries, keys, values, segments.reshape(1, TOK))


def attend_kernel(steps, sinks, pack_ref, low_ref, out_ref, key_a, key_b, val_a, val_b, doc_row, bias, hold):
    ctx = lax.axis_index("ctx")
    y, x = ctx // NX, lax.rem(ctx, NX)
    lane = lax.broadcasted_iota(jnp.int32, (TOK, 128), 1)

    def place(ref, b, first, slot):
        rows = pl.ds(pl.multiple_of(slot * TOK, TOK), TOK)
        keys = ref[b, 0:TOK, first : first + 128].astype(jnp.float32)
        vals = ref[b, 0:TOK, first + 128 : first + 256].astype(jnp.float32)
        for g in range(2):
            mine = (lane < 64) if g == 0 else (lane >= 64)
            k_here = jnp.where(mine, keys, 0.0)
            v_here = jnp.where(mine, vals, 1.0)
            k_roll = pltpu.roll(k_here, 64, 1)
            v_roll = pltpu.roll(v_here, 64, 1)
            pair_k = (k_here, k_roll) if g == 0 else (k_roll, k_here)
            pair_v = (v_here, v_roll) if g == 0 else (v_roll, v_here)
            key_a[g, rows] = pair_k[0].astype(jnp.bfloat16)
            key_b[g, rows] = pair_k[1].astype(jnp.bfloat16)
            val_a[g, rows] = pair_v[0].astype(jnp.bfloat16)
            val_b[g, rows] = pair_v[1].astype(jnp.bfloat16)
        doc_row[:, rows] = ref[b, TOK : TOK + 8, first : first + 128].astype(jnp.float32)

    for b in range(NX):
        place(pack_ref, b, 1024, 4 * y + b)

    @pl.when(y == 1)
    def _():
        for b in range(NX):
            place(low_ref, b, 0, b)

    two = 2 * TOK
    upper = lax.broadcasted_iota(jnp.int32, (two, 128), 0) < TOK
    first = lax.broadcasted_iota(jnp.int32, (two, 128), 1) < 64

    for index, step in enumerate(steps):
        j = lax.rem(x + step, NX)
        block = 4 * y + j
        own_docs = doc_row[0:1, pl.ds(pl.multiple_of(block * TOK, TOK), TOK)]
        query_docs = jnp.transpose(jnp.broadcast_to(own_docs, (TOK, TOK)))
        query_place = block * TOK + lax.broadcasted_iota(jnp.int32, (TOK, 128), 0)

        def run(chunks, index=index, j=j, query_docs=query_docs, query_place=query_place):
            for t in range(2 * chunks):
                cols = slice(128 * t, 128 * t + 128)
                allowed = (query_docs == doc_row[0:1, cols]) & (128 * t + lane <= query_place)
                bias[:, cols] = jnp.where(allowed, 0.0, -jnp.inf)

            def quad(p, carry):
                g = p // 2
                base = pl.multiple_of(p * 256, 256)
                place_out = pl.multiple_of(512 * lax.rem(g + y, 2) + 256 * lax.rem(p, 2), 256)
                q = jnp.concatenate(
                    [
                        pack_ref[j, 0:TOK, pl.ds(base, 128)],
                        pack_ref[j, 0:TOK, pl.ds(pl.multiple_of(base + 128, 128), 128)],
                    ],
                    axis=0,
                )
                head = 8 * x + 32 * g + 4 * lax.rem(p, 2)
                tops, sink_rows = [], []
                for which, key_ref in enumerate((key_a, key_b)):
                    sink = jnp.where(upper, sinks[head + which], sinks[head + 2 + which])
                    top = sink
                    for c in range(chunks):
                        cols = slice(256 * c, 256 * c + 256)
                        s = lax.dot_general(
                            q, key_ref[g, cols], NT, preferred_element_type=jnp.float32
                        )
                        mask = bias[:, cols]
                        s = s + jnp.concatenate([mask, mask], axis=0)
                        hold[which, :, cols] = s
                        top = jnp.maximum(top, jnp.maximum(s[:, 0:128], s[:, 128:256]))
                    tops.append(jnp.max(top, axis=1, keepdims=True))
                    sink_rows.append(sink)
                outs = []
                for which, val_ref in enumerate((val_a, val_b)):
                    total = jnp.zeros((two, 128), jnp.float32)
                    for c in range(chunks):
                        cols = slice(256 * c, 256 * c + 256)
                        prob = jnp.exp(hold[which, :, cols] - tops[which]).astype(jnp.bfloat16)
                        total = total + jnp.dot(
                            prob, val_ref[g, cols], preferred_element_type=jnp.float32
                        )
                    outs.append(total)
                numer = jnp.where(first, outs[0], outs[1])
                divisor = pltpu.roll(jnp.where(first, outs[1], outs[0]), 64, 1)
                gap = jnp.where(first, sink_rows[0] - tops[0], sink_rows[1] - tops[1])
                result = (numer / (divisor + jnp.exp(gap))).astype(jnp.bfloat16)
                rows = slice(index * TOK, index * TOK + TOK)
                out_ref[rows, pl.ds(place_out, 128)] = result[0:TOK]
                out_ref[rows, pl.ds(pl.multiple_of(place_out + 128, 128), 128)] = result[TOK:]
                return carry

            lax.fori_loop(0, 4, quad, 0)

        for quarter in range(4):

            @pl.when(block // 2 == quarter)
            def _(run=run, quarter=quarter):
                run(quarter + 1)


def attend(steps, sinks, packed, low):
    return pl.pallas_call(
        functools.partial(attend_kernel, steps),
        out_shape=jax.ShapeDtypeStruct((2 * TOK, 1024), jnp.bfloat16),
        in_specs=[spec(SMEM), spec(VMEM), spec(VMEM)],
        out_specs=spec(VMEM),
        scratch_shapes=[
            pltpu.VMEM((2, 1024, 128), jnp.bfloat16),
            pltpu.VMEM((2, 1024, 128), jnp.bfloat16),
            pltpu.VMEM((2, 1024, 128), jnp.bfloat16),
            pltpu.VMEM((2, 1024, 128), jnp.bfloat16),
            pltpu.VMEM((8, 1024), jnp.float32),
            pltpu.VMEM((TOK, 1024), jnp.float32),
            pltpu.VMEM((2, 2 * TOK, 1024), jnp.float32),
        ],
        compiler_params=params(20),
        cost_estimate=pl.CostEstimate(
            flops=2 << 30, bytes_accessed=4 << 20, transcendentals=0
        ),
    )(sinks, packed, low)


def project_kernel(finish, attn, w_own, w_first, w_second, *refs):
    core = lax.rem(lax.axis_index("exp"), 2)
    if finish:
        plus_a, ra, lb = refs[:3]
        to_right, left_a, left_b, right_a, right_b = refs[3:]
        to_right[...] = add(plus_a[...], ra[...])
    else:
        left_a, left_b, right_a, right_b = refs
    for w_near, base, left_out, right_out in (
        (w_first, core * HALF, left_a, right_a),
        (w_second, (1 - core) * HALF, left_b, right_b),
    ):
        for start in range(0, HALF, 288):
            near = slice(start, start + 288)
            rows = pl.ds(pl.multiple_of(base + start, 16), 288)
            total = lax.dot_general(
                w_own[rows], attn[:, 0:512], NT, preferred_element_type=jnp.float32
            ) + lax.dot_general(
                w_near[near], attn[:, 512:1024], NT, preferred_element_type=jnp.float32
            )
            left = total[:, 0:128]
            if finish and left_out is left_b:
                left = left + lb[near].astype(jnp.float32)
            left_out[near] = left.astype(jnp.bfloat16)
            right_out[near] = total[:, 128:256].astype(jnp.bfloat16)


def project(attn, w_own, w_first, w_second, *extra):
    finish = len(extra) > 0
    count = 5 if finish else 4
    return pl.pallas_call(
        functools.partial(project_kernel, finish),
        out_shape=(jax.ShapeDtypeStruct((HALF, TOK), jnp.bfloat16),) * count,
        in_specs=[spec(VMEM)] * (4 + len(extra)),
        out_specs=(spec(VMEM),) * count,
        compiler_params=params(20),
        cost_estimate=pl.CostEstimate(flops=3 << 29, bytes_accessed=4 << 20, transcendentals=0),
    )(attn, w_own, w_first, w_second, *extra)


def slot_table(ids):
    local = ids % QUARTER
    chosen = jnp.where(local < WINDOW, ids // QUARTER * WINDOW + local, -1)
    slot = lax.broadcasted_iota(jnp.int32, (TOK, TOK), 0)
    expert = slot // CAP
    hits = [chosen[k : k + 1] == expert for k in range(TOPK)]
    named = functools.reduce(jnp.logical_or, hits)
    before = lax.broadcasted_iota(jnp.int32, (TOK, TOK), 0) < lax.broadcasted_iota(
        jnp.int32, (TOK, TOK), 1
    )
    rank = jnp.dot(
        jnp.where(named, 1.0, 0.0).astype(jnp.bfloat16),
        jnp.where(before, 1.0, 0.0).astype(jnp.bfloat16),
        preferred_element_type=jnp.float32,
    )
    table = named & (rank == (slot % CAP).astype(jnp.float32))
    return table, hits


def norm_kernel(
    resid, own_a, own_b, left_a, left_b, right_a, right_b, gain, ids, hidden_ref, send_ref, gain_row
):
    core = lax.rem(lax.axis_index("exp"), 2)
    gain_row[...] = jnp.ones_like(gain_row)
    gain_row[:, 0:D] = gain[...]
    square = jnp.zeros((8, TOK), jnp.float32)
    for base, own, left, right in (
        (core * HALF, own_a, left_a, right_a),
        ((1 - core) * HALF, own_b, left_b, right_b),
    ):
        for start in range(0, HALF, 160):
            near = slice(start, start + 160)
            rows = pl.ds(pl.multiple_of(base + start, 16), 160)
            total = own[near].astype(jnp.float32)
            total = total + left[near].astype(jnp.float32) + right[near].astype(jnp.float32)
            hidden = resid[rows].astype(jnp.float32) + total
            hidden_ref[rows] = hidden
            square = square + jnp.sum((hidden * hidden).reshape(20, 8, TOK), axis=0)
    mean = jnp.sum(square, axis=0, keepdims=True) * (1.0 / D)
    scale = lax.rsqrt(mean + 1e-05)
    table, _ = slot_table(ids[...])
    table = jnp.where(table, 1.0, 0.0).astype(jnp.bfloat16)
    for start in range(0, D, 128):
        size = min(128, D - start)
        rows = slice(start, start + size)
        gains = jnp.transpose(jnp.broadcast_to(gain_row[:, start : start + 128], (128, 128)))
        normed = (hidden_ref[rows] * scale * gains[0:size]).astype(jnp.bfloat16)
        send_ref[:, rows] = lax.dot_general(
            table, normed, NT, preferred_element_type=jnp.float32
        ).astype(jnp.bfloat16)


def norm(resid, own_a, own_b, left_a, left_b, right_a, right_b, gain, ids):
    return pl.pallas_call(
        norm_kernel,
        out_shape=(
            jax.ShapeDtypeStruct((D, TOK), jnp.float32),
            jax.ShapeDtypeStruct((TOK, D), jnp.bfloat16),
        ),
        in_specs=[spec(VMEM)] * 9,
        out_specs=(spec(VMEM), spec(VMEM)),
        scratch_shapes=[pltpu.VMEM((1, D + 64), jnp.float32)],
        compiler_params=params(16),
        cost_estimate=pl.CostEstimate(flops=1 << 27, bytes_accessed=6 << 20, transcendentals=0),
    )(resid, own_a, own_b, left_a, left_b, right_a, right_b, gain, ids)


def combine_kernel(hidden, back, ids, weights, out_ref):
    table, hits = slot_table(ids[...])
    chosen_weight = jnp.zeros((TOK, TOK), jnp.float32)
    for k in range(TOPK):
        chosen_weight = chosen_weight + jnp.where(hits[k], weights[k : k + 1], 0.0)
    share = jnp.where(table, chosen_weight, 0.0)
    high = share.astype(jnp.bfloat16)
    low = (share - high.astype(jnp.float32)).astype(jnp.bfloat16)
    for start in range(0, D, 128):
        cols = slice(start, min(start + 128, D))
        rows = back[:, cols]
        moe = lax.dot_general(rows, high, TN, preferred_element_type=jnp.float32)
        moe = moe + lax.dot_general(rows, low, TN, preferred_element_type=jnp.float32)
        out_ref[cols] = (hidden[cols] + moe).astype(jnp.bfloat16)


def combine(hidden, back, ids, weights):
    return pl.pallas_call(
        combine_kernel,
        out_shape=jax.ShapeDtypeStruct((D, TOK), jnp.bfloat16),
        in_specs=[spec(VMEM)] * 4,
        out_specs=spec(VMEM),
        compiler_params=params(16),
        cost_estimate=pl.CostEstimate(flops=1 << 28, bytes_accessed=3 << 20, transcendentals=0),
    )(hidden, back, ids, weights)


LOADS = ((2, 3), (4, 5), (7, 8))


def expert_kernel(sizes, *refs):
    count = len(sizes)
    pieces, weights, outs = refs[:count], refs[count : count + 9], refs[count + 9 : 2 * count + 9]
    rows_x, held, sem = refs[2 * count + 9], refs[2 * count + 10 : 2 * count + 13], refs[-1]
    core = lax.rem(lax.axis_index("exp"), 2)
    copies = []
    start = 0
    for index, (piece, size) in enumerate(zip(pieces, sizes)):
        copies.append(
            pltpu.make_async_copy(piece, rows_x.at[pl.ds(start, size)], sem.at[index])
        )
        start += size
    loads = []
    for index, (group, dst) in enumerate(zip(LOADS, held)):
        loads.append(
            [pltpu.make_async_copy(weights[w], dst, sem.at[count + index]) for w in group]
        )

    def each(load, act):
        for which, copy in enumerate(load):

            @pl.when(core == which)
            def _(copy=copy):
                act(copy)

    def start_load(load):
        each(load, lambda copy: copy.start())

    def wait_load(load):
        each(load, lambda copy: copy.wait())

    for copy in copies:
        copy.start()
    for load in loads:
        start_load(load)
    for copy in copies:
        copy.wait()
    x = rows_x[...]
    gate_own, up_own, down_own = weights[0], weights[1], weights[6]
    gate_near, up_near, down_near = held

    def hidden_units(gate, up, ready):
        g = lax.dot_general(x, gate[...], NT, preferred_element_type=jnp.float32)
        ready()
        v = lax.dot_general(x, up[...], NT, preferred_element_type=jnp.float32)
        return ((v + 1.0) * g * jax.nn.sigmoid(1.702 * g)).astype(jnp.bfloat16)

    act_own = hidden_units(gate_own, up_own, lambda: None)
    wait_load(loads[0])
    act_near = hidden_units(gate_near, up_near, lambda: wait_load(loads[1]))
    wait_load(loads[2])
    for first in range(0, D, 512):
        cols = slice(first, min(first + 512, D))
        part = jnp.dot(act_own, down_own[:, cols], preferred_element_type=jnp.float32)
        part = part + jnp.dot(act_near, down_near[:, cols], preferred_element_type=jnp.float32)
        part = part.astype(jnp.bfloat16)
        start = 0
        for out, size in zip(outs, sizes):
            out[:, cols] = part[start : start + size]
            start += size


def experts(pieces, weights):
    sizes = tuple(piece.shape[0] for piece in pieces)
    total = sum(sizes)
    return pl.pallas_call(
        functools.partial(expert_kernel, sizes),
        out_shape=tuple(jax.ShapeDtypeStruct((size, D), jnp.bfloat16) for size in sizes),
        in_specs=[spec(ANY)] * len(sizes)
        + [spec(VMEM)] * 2
        + [spec(ANY)] * 4
        + [spec(VMEM)]
        + [spec(ANY)] * 2,
        out_specs=tuple(spec(VMEM) for _ in sizes),
        scratch_shapes=[pltpu.VMEM((total, D), jnp.bfloat16)]
        + [pltpu.VMEM((FFS, D), jnp.bfloat16)] * 3
        + [pltpu.SemaphoreType.DMA((len(sizes) + 3,))],
        compiler_params=params(32),
        cost_estimate=pl.CostEstimate(
            flops=12 * total * D * FFS, bytes_accessed=14 << 20, transcendentals=2 * total * FFS
        ),
    )(*pieces, *weights)


def over_all(move):
    pairs = []
    for c in range(8):
        for e in range(16):
            y, x, z, hi, core = move(c // 4, c % 4, e // 4, e // 2 % 2, e % 2)
            pairs.append((c * 16 + e, (y * 4 + x) * 16 + z * 4 + hi * 2 + core))
    return pairs


def partner(y, x, z, hi, core):
    return (1 - y, x, z, hi, core) if core == 0 else (y, x ^ 1, z, hi, core)


def onward(y, x, z, hi, core):
    if core == 0:
        return y, (x + 1) % 4, z, hi, core
    across = x < 2 if y == 0 else x >= 2
    return (y, 3 - x, z, hi, core) if across else (1 - y, x, z, hi, core)


def across_y(y, x, z, hi, core):
    place = (2 * hi + y + (1 if y == 1 else 3)) % 4
    return place % 2, x, z, place // 2, core


def permute(v, pairs):
    return lax.ppermute(v, ("ctx", "exp"), pairs)


NEXT = over_all(onward)
BACK = [(b, a) for a, b in NEXT]
PARTNER = [[(a, b) for a, b in over_all(partner) if a % 2 == core] for core in range(2)]
ACROSS = over_all(across_y)
SWAP = over_all(lambda y, x, z, hi, core: (y, x, z, hi, 1 - core))


def exchange_experts(arrived, weights):
    half = TOK // 2
    own_a, own_b = arrived[:half], arrived[half:]
    prev_a, next_b = permute(own_a, NEXT), permute(own_b, BACK)
    prev_b, next_a = permute(own_b, NEXT), permute(own_a, BACK)
    opp_a, opp_b = permute(prev_a, NEXT), permute(next_b, BACK)
    oo_a, oo_b, op_a, op_b, on_a, on_b = experts(
        (own_a, own_b, prev_a, prev_b, next_a, next_b), weights
    )
    opp_a, opp_b, oo_a, oo_b, op_a, op_b, on_a, on_b = lax.optimization_barrier(
        (opp_a, opp_b, oo_a, oo_b, op_a, op_b, on_a, on_b)
    )
    far_a, far_b = experts((opp_a, opp_b), weights)
    on_at_next, op_at_prev = permute(far_a, NEXT), permute(far_b, BACK)
    got_b, got_a = permute(on_b, NEXT), permute(op_a, BACK)
    more_a = permute(add(on_a, on_at_next), NEXT)
    more_b = permute(add(op_b, op_at_prev), BACK)
    return jnp.concatenate([add(oo_a, got_a, more_a), add(oo_b, got_b, more_b)], axis=0)


def on_device(
    resid_in,
    queries,
    keys,
    values,
    sinks,
    segments,
    norm_gain,
    out_weight,
    gate_weight,
    up_weight,
    down_weight,
    expert_ids,
    route_weights,
):
    core = lax.axis_index("exp") % 2
    gate, up, down = gate_weight[0].T, up_weight[0].T, down_weight[0]
    w_own = out_weight.T

    mine = lax.dynamic_slice_in_dim(w_own, core * (D // 2), D // 2, 0)
    w_first = permute(mine, ACROSS)
    gate_0 = permute(gate, PARTNER[0])

    packed = pack(queries, keys, values, segments)
    packed = lax.all_to_all(
        packed,
        "ctx",
        split_axis=0,
        concat_axis=0,
        tiled=True,
        axis_index_groups=[[0, 1, 2, 3], [4, 5, 6, 7]],
    )
    packed, gate_0, gate_out = lax.optimization_barrier((packed, gate_0, gate))
    low = lax.ppermute(packed[:, :, 1024:], "ctx", [(x, x + 4) for x in range(4)])
    gate_1 = permute(gate_out, PARTNER[1])
    low, w_first, up_out, down_out = lax.optimization_barrier((low, w_first, up, down))
    w_second = permute(w_first, SWAP)
    up_0, down_0 = permute(up_out, PARTNER[0]), permute(down_out, PARTNER[0])

    attn = attend((2, 1), sinks, packed, low)
    opp_a, opp_b, plus_a, plus_b = project(attn, w_own, w_first, w_second)
    ra, lb, right_b = go_right(opp_a), go_left(opp_b), go_right(plus_b)
    attn = attend((3, 0), sinks, packed, low)
    attn, gate_1, up_0 = lax.optimization_barrier((attn, gate_1, up_0))
    to_right, to_left_a, to_left_b, own_a, own_b = project(
        attn, w_own, w_first, w_second, plus_a, ra, lb
    )
    right_a, left_a, left_b = go_right(to_right), go_left(to_left_a), go_left(to_left_b)

    right_a, right_b, left_a, left_b, up_out, down_out = lax.optimization_barrier(
        (right_a, right_b, left_a, left_b, up, down)
    )
    up_1, down_1 = permute(up_out, PARTNER[1]), permute(down_out, PARTNER[1])

    ids = expert_ids.T
    hidden, send = norm(
        resid_in.T, own_a, own_b, right_a, right_b, left_a, left_b, norm_gain.reshape(1, D), ids
    )
    send, down_0 = lax.optimization_barrier((send, down_0))
    arrived = lax.all_to_all(send, "exp", split_axis=0, concat_axis=0, tiled=True)
    arrived, up_1 = lax.optimization_barrier((arrived, up_1))
    summed = exchange_experts(
        arrived, (gate, up, gate_0, gate_1, up_0, up_1, down, down_0, down_1)
    )
    back = lax.all_to_all(summed, "exp", split_axis=0, concat_axis=0, tiled=True)
    return combine(hidden, back, ids, route_weights.T).T


def solution(mesh):
    placed = (
        P(("exp", "ctx"), None),
        P(("exp", "ctx"), None),
        P(("exp", "ctx"), None),
        P(("exp", "ctx"), None),
        P(),
        P(("exp", "ctx")),
        P(),
        P("ctx", None),
        P("exp", None, "ctx"),
        P("exp", None, "ctx"),
        P("exp", "ctx", None),
        P(("exp", "ctx"), None),
        P(("exp", "ctx"), None),
    )
    return jax.shard_map(
        on_device, mesh=mesh, in_specs=placed, out_specs=P(("exp", "ctx"), None), check_vma=False
    )
```

```python
import functools

import jax
import jax.numpy as jnp
from jax import lax
from jax.experimental import pallas as pl
from jax.experimental.pallas import tpu as pltpu
from jax.sharding import PartitionSpec as P

D = 2880
QUERY_HEADS = 64
KEY_VALUE_HEADS = 8
HEAD_SIZE = 64
ALL_EXPERTS = 128
TOPK = 4
CAP = 8
TOK = 128
FFS = 360
NX = 4
QUARTER = ALL_EXPERTS // TOPK
WINDOW = 4
DOC_ROWS = 16
PACK_ROWS = TOK + DOC_ROWS
PACK_COLS = 1280
HALF = D // 2
MIB = 1024 * 1024

VMEM = pltpu.VMEM
ANY = pl.ANY
SMEM = pltpu.SMEM

RIGHT = [(4 * y + x, 4 * y + (x + 1) % 4) for y in range(2) for x in range(4)]
LEFT = [(4 * y + x, 4 * y + (x + 3) % 4) for y in range(2) for x in range(4)]
FLIP = [(c, c ^ 4) for c in range(8)]

NT = (((1,), (1,)), ((), ()))
TN = (((0,), (0,)), ((), ()))


def go_right(v):
    return lax.ppermute(v, "ctx", RIGHT)


def go_left(v):
    return lax.ppermute(v, "ctx", LEFT)


def go_flip(v):
    return lax.ppermute(v, "ctx", FLIP)


def params(mib):
    return pltpu.CompilerParams(vmem_limit_bytes=mib * MIB)


def spec(space):
    return pl.BlockSpec(memory_space=space)


def add(*pieces):
    total = pieces[0].astype(jnp.float32)
    for piece in pieces[1:]:
        total = total + piece.astype(jnp.float32)
    return total.astype(jnp.bfloat16)


def pack_kernel(q_ref, k_ref, v_ref, seg_ref, out_ref):
    lane = lax.broadcasted_iota(jnp.int32, (TOK, 128), 1)
    docs = jnp.broadcast_to(seg_ref[...].astype(jnp.float32), (DOC_ROWS, 128))
    eighth = jnp.asarray(0.125, jnp.bfloat16)
    for x in range(NX):
        out_ref[x, :TOK, 0:512] = q_ref[:, 512 * x : 512 * x + 512] * eighth
        out_ref[x, :TOK, 512:1024] = q_ref[:, 2048 + 512 * x : 2048 + 512 * x + 512] * eighth
        for ref, start in ((k_ref, 1024), (v_ref, 1152)):
            base = 128 * (x // 2)
            low = ref[:, base : base + 128].astype(jnp.float32)
            high = ref[:, 256 + base : 256 + base + 128].astype(jnp.float32)
            if x % 2 == 0:
                high = pltpu.roll(high, 64, 1)
            else:
                low = pltpu.roll(low, 64, 1)
            out_ref[x, :TOK, start : start + 128] = jnp.where(lane < 64, low, high).astype(
                jnp.bfloat16
            )
        out_ref[x, TOK:, 0:1024] = jnp.zeros((DOC_ROWS, 1024), jnp.bfloat16)
        out_ref[x, TOK:, 1024:1152] = docs.astype(jnp.bfloat16)
        out_ref[x, TOK:, 1152:1280] = jnp.zeros((DOC_ROWS, 128), jnp.bfloat16)


def pack(queries, keys, values, segments):
    return pl.pallas_call(
        pack_kernel,
        out_shape=jax.ShapeDtypeStruct((NX, PACK_ROWS, PACK_COLS), jnp.bfloat16),
        in_specs=[spec(VMEM)] * 4,
        out_specs=spec(VMEM),
        compiler_params=params(12),
        cost_estimate=pl.CostEstimate(flops=0, bytes_accessed=5 << 20, transcendentals=0),
    )(queries, keys, values, segments.reshape(1, TOK))


def attend_kernel(steps, sinks, pack_ref, low_ref, out_ref, key_a, key_b, val_a, val_b, doc_row, bias, hold):
    ctx = lax.axis_index("ctx")
    y, x = ctx // NX, lax.rem(ctx, NX)
    lane = lax.broadcasted_iota(jnp.int32, (TOK, 128), 1)

    def place(ref, b, first, slot):
        rows = pl.ds(pl.multiple_of(slot * TOK, TOK), TOK)
        keys = ref[b, 0:TOK, first : first + 128].astype(jnp.float32)
        vals = ref[b, 0:TOK, first + 128 : first + 256].astype(jnp.float32)
        for g in range(2):
            mine = (lane < 64) if g == 0 else (lane >= 64)
            k_here = jnp.where(mine, keys, 0.0)
            v_here = jnp.where(mine, vals, 1.0)
            k_roll = pltpu.roll(k_here, 64, 1)
            v_roll = pltpu.roll(v_here, 64, 1)
            pair_k = (k_here, k_roll) if g == 0 else (k_roll, k_here)
            pair_v = (v_here, v_roll) if g == 0 else (v_roll, v_here)
            key_a[g, rows] = pair_k[0].astype(jnp.bfloat16)
            key_b[g, rows] = pair_k[1].astype(jnp.bfloat16)
            val_a[g, rows] = pair_v[0].astype(jnp.bfloat16)
            val_b[g, rows] = pair_v[1].astype(jnp.bfloat16)
        doc_row[:, rows] = ref[b, TOK : TOK + 8, first : first + 128].astype(jnp.float32)

    for b in range(NX):
        place(pack_ref, b, 1024, 4 * y + b)

    @pl.when(y == 1)
    def _():
        for b in range(NX):
            place(low_ref, b, 0, b)

    two = 2 * TOK
    upper = lax.broadcasted_iota(jnp.int32, (two, 128), 0) < TOK
    first = lax.broadcasted_iota(jnp.int32, (two, 128), 1) < 64

    for index, step in enumerate(steps):
        j = lax.rem(x + step, NX)
        block = 4 * y + j
        own_docs = doc_row[0:1, pl.ds(pl.multiple_of(block * TOK, TOK), TOK)]
        query_docs = jnp.transpose(jnp.broadcast_to(own_docs, (TOK, TOK)))
        query_place = block * TOK + lax.broadcasted_iota(jnp.int32, (TOK, 128), 0)

        def run(chunks, index=index, j=j, query_docs=query_docs, query_place=query_place):
            for t in range(2 * chunks):
                cols = slice(128 * t, 128 * t + 128)
                allowed = (query_docs == doc_row[0:1, cols]) & (128 * t + lane <= query_place)
                bias[:, cols] = jnp.where(allowed, 0.0, -jnp.inf)

            def quad(p, carry):
                g = p // 2
                base = pl.multiple_of(p * 256, 256)
                place_out = pl.multiple_of(512 * lax.rem(g + y, 2) + 256 * lax.rem(p, 2), 256)
                q = jnp.concatenate(
                    [
                        pack_ref[j, 0:TOK, pl.ds(base, 128)],
                        pack_ref[j, 0:TOK, pl.ds(pl.multiple_of(base + 128, 128), 128)],
                    ],
                    axis=0,
                )
                head = 8 * x + 32 * g + 4 * lax.rem(p, 2)
                tops, sink_rows = [], []
                for which, key_ref in enumerate((key_a, key_b)):
                    sink = jnp.where(upper, sinks[head + which], sinks[head + 2 + which])
                    top = sink
                    for c in range(chunks):
                        cols = slice(256 * c, 256 * c + 256)
                        s = lax.dot_general(
                            q, key_ref[g, cols], NT, preferred_element_type=jnp.float32
                        )
                        mask = bias[:, cols]
                        s = s + jnp.concatenate([mask, mask], axis=0)
                        hold[which, :, cols] = s
                        top = jnp.maximum(top, jnp.maximum(s[:, 0:128], s[:, 128:256]))
                    tops.append(jnp.max(top, axis=1, keepdims=True))
                    sink_rows.append(sink)
                outs = []
                for which, val_ref in enumerate((val_a, val_b)):
                    total = jnp.zeros((two, 128), jnp.float32)
                    for c in range(chunks):
                        cols = slice(256 * c, 256 * c + 256)
                        prob = jnp.exp(hold[which, :, cols] - tops[which]).astype(jnp.bfloat16)
                        total = total + jnp.dot(
                            prob, val_ref[g, cols], preferred_element_type=jnp.float32
                        )
                    outs.append(total)
                numer = jnp.where(first, outs[0], outs[1])
                divisor = pltpu.roll(jnp.where(first, outs[1], outs[0]), 64, 1)
                gap = jnp.where(first, sink_rows[0] - tops[0], sink_rows[1] - tops[1])
                result = (numer / (divisor + jnp.exp(gap))).astype(jnp.bfloat16)
                rows = slice(index * TOK, index * TOK + TOK)
                out_ref[rows, pl.ds(place_out, 128)] = result[0:TOK]
                out_ref[rows, pl.ds(pl.multiple_of(place_out + 128, 128), 128)] = result[TOK:]
                return carry

            lax.fori_loop(0, 4, quad, 0)

        for quarter in range(4):

            @pl.when(block // 2 == quarter)
            def _(run=run, quarter=quarter):
                run(quarter + 1)


def attend(steps, sinks, packed, low):
    return pl.pallas_call(
        functools.partial(attend_kernel, steps),
        out_shape=jax.ShapeDtypeStruct((2 * TOK, 1024), jnp.bfloat16),
        in_specs=[spec(SMEM), spec(VMEM), spec(VMEM)],
        out_specs=spec(VMEM),
        scratch_shapes=[
            pltpu.VMEM((2, 1024, 128), jnp.bfloat16),
            pltpu.VMEM((2, 1024, 128), jnp.bfloat16),
            pltpu.VMEM((2, 1024, 128), jnp.bfloat16),
            pltpu.VMEM((2, 1024, 128), jnp.bfloat16),
            pltpu.VMEM((8, 1024), jnp.float32),
            pltpu.VMEM((TOK, 1024), jnp.float32),
            pltpu.VMEM((2, 2 * TOK, 1024), jnp.float32),
        ],
        compiler_params=params(20),
        cost_estimate=pl.CostEstimate(
            flops=2 << 30, bytes_accessed=4 << 20, transcendentals=0
        ),
    )(sinks, packed, low)


def project_kernel(finish, attn, w_own, w_first, w_second, *refs):
    core = lax.rem(lax.axis_index("exp"), 2)
    if finish:
        plus_a, ra, lb = refs[:3]
        to_right, left_a, left_b, right_a, right_b = refs[3:]
        to_right[...] = add(plus_a[...], ra[...])
    else:
        left_a, left_b, right_a, right_b = refs
    for w_near, base, left_out, right_out in (
        (w_first, core * HALF, left_a, right_a),
        (w_second, (1 - core) * HALF, left_b, right_b),
    ):
        for start in range(0, HALF, 288):
            near = slice(start, start + 288)
            rows = pl.ds(pl.multiple_of(base + start, 16), 288)
            total = lax.dot_general(
                w_own[rows], attn[:, 0:512], NT, preferred_element_type=jnp.float32
            ) + lax.dot_general(
                w_near[near], attn[:, 512:1024], NT, preferred_element_type=jnp.float32
            )
            left = total[:, 0:128]
            if finish and left_out is left_b:
                left = left + lb[near].astype(jnp.float32)
            left_out[near] = left.astype(jnp.bfloat16)
            right_out[near] = total[:, 128:256].astype(jnp.bfloat16)


def project(attn, w_own, w_first, w_second, *extra):
    finish = len(extra) > 0
    count = 5 if finish else 4
    return pl.pallas_call(
        functools.partial(project_kernel, finish),
        out_shape=(jax.ShapeDtypeStruct((HALF, TOK), jnp.bfloat16),) * count,
        in_specs=[spec(VMEM)] * (4 + len(extra)),
        out_specs=(spec(VMEM),) * count,
        compiler_params=params(20),
        cost_estimate=pl.CostEstimate(flops=3 << 29, bytes_accessed=4 << 20, transcendentals=0),
    )(attn, w_own, w_first, w_second, *extra)


def slot_table(ids):
    local = ids % QUARTER
    chosen = jnp.where(local < WINDOW, ids // QUARTER * WINDOW + local, -1)
    slot = lax.broadcasted_iota(jnp.int32, (TOK, TOK), 0)
    expert = slot // CAP
    hits = [chosen[k : k + 1] == expert for k in range(TOPK)]
    named = functools.reduce(jnp.logical_or, hits)
    before = lax.broadcasted_iota(jnp.int32, (TOK, TOK), 0) < lax.broadcasted_iota(
        jnp.int32, (TOK, TOK), 1
    )
    rank = jnp.dot(
        jnp.where(named, 1.0, 0.0).astype(jnp.bfloat16),
        jnp.where(before, 1.0, 0.0).astype(jnp.bfloat16),
        preferred_element_type=jnp.float32,
    )
    table = named & (rank == (slot % CAP).astype(jnp.float32))
    return table, hits


def norm_kernel(
    resid, own_a, own_b, left_a, left_b, right_a, right_b, gain, ids, hidden_ref, send_ref, gain_row
):
    core = lax.rem(lax.axis_index("exp"), 2)
    gain_row[...] = jnp.ones_like(gain_row)
    gain_row[:, 0:D] = gain[...]
    square = jnp.zeros((8, TOK), jnp.float32)
    for base, own, left, right in (
        (core * HALF, own_a, left_a, right_a),
        ((1 - core) * HALF, own_b, left_b, right_b),
    ):
        for start in range(0, HALF, 160):
            near = slice(start, start + 160)
            rows = pl.ds(pl.multiple_of(base + start, 16), 160)
            total = own[near].astype(jnp.float32)
            total = total + left[near].astype(jnp.float32) + right[near].astype(jnp.float32)
            hidden = resid[rows].astype(jnp.float32) + total
            hidden_ref[rows] = hidden
            square = square + jnp.sum((hidden * hidden).reshape(20, 8, TOK), axis=0)
    mean = jnp.sum(square, axis=0, keepdims=True) * (1.0 / D)
    scale = lax.rsqrt(mean + 1e-05)
    table, _ = slot_table(ids[...])
    table = jnp.where(table, 1.0, 0.0).astype(jnp.bfloat16)
    for start in range(0, D, 128):
        size = min(128, D - start)
        rows = slice(start, start + size)
        gains = jnp.transpose(jnp.broadcast_to(gain_row[:, start : start + 128], (128, 128)))
        normed = (hidden_ref[rows] * scale * gains[0:size]).astype(jnp.bfloat16)
        send_ref[:, rows] = lax.dot_general(
            table, normed, NT, preferred_element_type=jnp.float32
        ).astype(jnp.bfloat16)


def norm(resid, own_a, own_b, left_a, left_b, right_a, right_b, gain, ids):
    return pl.pallas_call(
        norm_kernel,
        out_shape=(
            jax.ShapeDtypeStruct((D, TOK), jnp.float32),
            jax.ShapeDtypeStruct((TOK, D), jnp.bfloat16),
        ),
        in_specs=[spec(VMEM)] * 9,
        out_specs=(spec(VMEM), spec(VMEM)),
        scratch_shapes=[pltpu.VMEM((1, D + 64), jnp.float32)],
        compiler_params=params(16),
        cost_estimate=pl.CostEstimate(flops=1 << 27, bytes_accessed=6 << 20, transcendentals=0),
    )(resid, own_a, own_b, left_a, left_b, right_a, right_b, gain, ids)


def combine_kernel(hidden, back, ids, weights, out_ref):
    table, hits = slot_table(ids[...])
    chosen_weight = jnp.zeros((TOK, TOK), jnp.float32)
    for k in range(TOPK):
        chosen_weight = chosen_weight + jnp.where(hits[k], weights[k : k + 1], 0.0)
    share = jnp.where(table, chosen_weight, 0.0)
    high = share.astype(jnp.bfloat16)
    low = (share - high.astype(jnp.float32)).astype(jnp.bfloat16)
    for start in range(0, D, 128):
        cols = slice(start, min(start + 128, D))
        rows = back[:, cols]
        moe = lax.dot_general(rows, high, TN, preferred_element_type=jnp.float32)
        moe = moe + lax.dot_general(rows, low, TN, preferred_element_type=jnp.float32)
        out_ref[cols] = (hidden[cols] + moe).astype(jnp.bfloat16)


def combine(hidden, back, ids, weights):
    return pl.pallas_call(
        combine_kernel,
        out_shape=jax.ShapeDtypeStruct((D, TOK), jnp.bfloat16),
        in_specs=[spec(VMEM)] * 4,
        out_specs=spec(VMEM),
        compiler_params=params(16),
        cost_estimate=pl.CostEstimate(flops=1 << 28, bytes_accessed=3 << 20, transcendentals=0),
    )(hidden, back, ids, weights)


def expert_kernel(sizes, plan, count_out, compute, *refs):
    count = len(sizes)
    total = max(max(group) for group in plan) + 1
    pieces, weights = refs[:count], refs[count : count + total]
    outs = refs[count + total : count + total + count_out]
    rows, held, sem = refs[count + total + count_out], refs[count + total + count_out + 1 : -1], refs[-1]
    core = lax.rem(lax.axis_index("exp"), 2)

    def load(index, act):
        group = plan[index]
        for which, source in enumerate(group):

            def go(source=source):
                act(pltpu.make_async_copy(weights[source], held[index], sem.at[count + index]))

            if len(group) == 1:
                go()
            else:
                pl.when(core == which)(go)

    copies = []
    start = 0
    for index, (piece, size) in enumerate(zip(pieces, sizes)):
        copies.append(pltpu.make_async_copy(piece, rows.at[pl.ds(start, size)], sem.at[index]))
        start += size
    for copy in copies:
        copy.start()
    for index in range(len(plan)):
        load(index, lambda copy: copy.start())
    for copy in copies:
        copy.wait()

    def weight(index):
        load(index, lambda copy: copy.wait())
        return held[index]

    compute(rows, weight, outs)


def expert_call(pieces, weights, plan, outs, compute, flops):
    sizes = tuple(piece.shape[0] for piece in pieces)
    return pl.pallas_call(
        functools.partial(expert_kernel, sizes, plan, len(outs), compute),
        out_shape=tuple(jax.ShapeDtypeStruct(shape, jnp.bfloat16) for shape in outs),
        in_specs=[spec(ANY)] * (len(sizes) + len(weights)),
        out_specs=tuple(spec(VMEM) for _ in outs),
        scratch_shapes=[pltpu.VMEM((sum(sizes), pieces[0].shape[1]), jnp.bfloat16)]
        + [pltpu.VMEM((FFS, D), jnp.bfloat16)] * len(plan)
        + [pltpu.SemaphoreType.DMA((len(sizes) + len(plan),))],
        compiler_params=params(24),
        cost_estimate=pl.CostEstimate(flops=flops, bytes_accessed=4 << 20, transcendentals=0),
    )(*pieces, *weights)


def act_compute(rows, weight, outs):
    x = rows[...]
    for part, out in enumerate(outs):
        g = lax.dot_general(x, weight(2 * part)[...], NT, preferred_element_type=jnp.float32)
        v = lax.dot_general(x, weight(2 * part + 1)[...], NT, preferred_element_type=jnp.float32)
        out[...] = ((v + 1.0) * g * jax.nn.sigmoid(1.702 * g)).astype(jnp.bfloat16)


def hidden_units(pieces, weights):
    rows = sum(piece.shape[0] for piece in pieces)
    return expert_call(
        pieces, weights, ((0,), (1,), (2, 3), (4, 5)), [(rows, FFS)] * 2, act_compute, 8 * rows * D * FFS
    )


def down_compute(rows, weight, outs):
    half = rows.shape[0] // 2
    own, near = rows[0:half], rows[half:]
    down_own, down_near = weight(0), weight(1)
    for first in range(0, D, 512):
        cols = slice(first, min(first + 512, D))
        part = jnp.dot(own, down_own[:, cols], preferred_element_type=jnp.float32)
        part = part + jnp.dot(near, down_near[:, cols], preferred_element_type=jnp.float32)
        part = part.astype(jnp.bfloat16)
        start = 0
        for out in outs:
            out[:, cols] = part[start : start + out.shape[0]]
            start += out.shape[0]


def from_hidden(acts, weights):
    rows = acts[0].shape[0]
    return expert_call(
        acts, weights, ((0,), (1, 2)), [(rows // 4, D)] * 4, down_compute, 4 * rows * D * FFS
    )


def over_all(move):
    pairs = []
    for c in range(8):
        for e in range(16):
            y, x, z, hi, core = move(c // 4, c % 4, e // 4, e // 2 % 2, e % 2)
            pairs.append((c * 16 + e, (y * 4 + x) * 16 + z * 4 + hi * 2 + core))
    return pairs


def partner(y, x, z, hi, core):
    return (1 - y, x, z, hi, core) if core == 0 else (y, x ^ 1, z, hi, core)


def onward(y, x, z, hi, core):
    if core == 0:
        return y, (x + 1) % 4, z, hi, core
    across = x < 2 if y == 0 else x >= 2
    return (y, 3 - x, z, hi, core) if across else (1 - y, x, z, hi, core)


def beside(y, x, z, hi, core):
    place = (2 * hi + y + (3 if core == 0 else 1)) % 4
    return place % 2, x, z, place // 2, core


def permute(v, pairs):
    return lax.ppermute(v, ("ctx", "exp"), pairs)


NEXT = over_all(onward)
BACK = [(b, a) for a, b in NEXT]
PARTNER = over_all(partner)
PARTNER_0 = [(a, b) for a, b in PARTNER if a % 2 == 0]
PARTNER_1 = [(a, b) for a, b in PARTNER if a % 2 == 1]
BESIDE = over_all(beside)
SWAP = over_all(lambda y, x, z, hi, core: (y, x, z, hi, 1 - core))


def exchange_experts(arrived, into, out_of):
    half = TOK // 2
    own_a, own_b = arrived[:half], arrived[half:]
    prev_a, next_b = permute(own_a, NEXT), permute(own_b, BACK)
    prev_b, next_a = permute(own_b, NEXT), permute(own_a, BACK)
    opp_a, opp_b = permute(prev_a, NEXT), permute(next_b, BACK)
    acts = hidden_units((own_a, own_b, prev_a, next_b), into)
    opp_a, opp_b, prev_b, next_a, acts = lax.optimization_barrier(
        (opp_a, opp_b, prev_b, next_a, acts)
    )
    oo_a, oo_b, op_a, on_b = from_hidden(acts, out_of)
    got_b, got_a = permute(on_b, NEXT), permute(op_a, BACK)
    acts = hidden_units((opp_a, opp_b, prev_b, next_a), into)
    far_a, far_b, op_b, on_a = from_hidden(acts, out_of)
    got_a, got_b, far_a, far_b, op_b, on_a = lax.optimization_barrier(
        (got_a, got_b, far_a, far_b, op_b, on_a)
    )
    more_a = permute(add(on_a, permute(far_a, NEXT)), NEXT)
    more_b = permute(add(op_b, permute(far_b, BACK)), BACK)
    return jnp.concatenate([add(oo_a, got_a, more_a), add(oo_b, got_b, more_b)], axis=0)


def on_device(
    resid_in,
    queries,
    keys,
    values,
    sinks,
    segments,
    norm_gain,
    out_weight,
    gate_weight,
    up_weight,
    down_weight,
    expert_ids,
    route_weights,
):
    core = lax.axis_index("exp") % 2
    gate, up, down = gate_weight[0].T, up_weight[0].T, down_weight[0]
    w_own = out_weight.T

    mine = lax.dynamic_slice_in_dim(w_own, core * (D // 2), D // 2, 0)
    w_first = permute(mine, BESIDE)

    packed = pack(queries, keys, values, segments)
    packed = lax.all_to_all(
        packed,
        "ctx",
        split_axis=0,
        concat_axis=0,
        tiled=True,
        axis_index_groups=[[0, 1, 2, 3], [4, 5, 6, 7]],
    )
    packed, w_first, gate_out = lax.optimization_barrier((packed, w_first, gate))
    low = lax.ppermute(packed[:, :, 1024:], "ctx", [(x, x + 4) for x in range(4)])
    gate_1 = permute(gate_out, PARTNER_1)
    w_second = permute(w_first, SWAP)
    low, gate_out = lax.optimization_barrier((low, gate))
    gate_0 = permute(gate_out, PARTNER_0)

    attn = attend((2, 1), sinks, packed, low)
    opp_a, opp_b, plus_a, plus_b = project(attn, w_own, w_first, w_second)
    ra, lb, right_b = go_right(opp_a), go_left(opp_b), go_right(plus_b)
    attn = attend((3, 0), sinks, packed, low)
    attn, ra, lb, right_b, gate_0, gate_1, up_out, down_out = lax.optimization_barrier(
        (attn, ra, lb, right_b, gate_0, gate_1, up, down)
    )
    up_0, down_0 = permute(up_out, PARTNER_0), permute(down_out, PARTNER_0)
    to_right, to_left_a, to_left_b, own_a, own_b = project(
        attn, w_own, w_first, w_second, plus_a, ra, lb
    )
    right_a, left_a, left_b = go_right(to_right), go_left(to_left_a), go_left(to_left_b)

    right_a, right_b, left_a, left_b, up_out, down_out = lax.optimization_barrier(
        (right_a, right_b, left_a, left_b, up, down)
    )
    up_1, down_1 = permute(up_out, PARTNER_1), permute(down_out, PARTNER_1)

    ids = expert_ids.T
    hidden, send = norm(
        resid_in.T, own_a, own_b, right_a, right_b, left_a, left_b, norm_gain.reshape(1, D), ids
    )
    send, up_0 = lax.optimization_barrier((send, up_0))
    arrived = lax.all_to_all(send, "exp", split_axis=0, concat_axis=0, tiled=True)
    arrived, down_0 = lax.optimization_barrier((arrived, down_0))
    summed = exchange_experts(
        arrived, (gate, up, gate_0, gate_1, up_0, up_1), (down, down_0, down_1)
    )
    back = lax.all_to_all(summed, "exp", split_axis=0, concat_axis=0, tiled=True)
    return combine(hidden, back, ids, route_weights.T).T


def solution(mesh):
    placed = (
        P(("exp", "ctx"), None),
        P(("exp", "ctx"), None),
        P(("exp", "ctx"), None),
        P(("exp", "ctx"), None),
        P(),
        P(("exp", "ctx")),
        P(),
        P("ctx", None),
        P("exp", None, "ctx"),
        P("exp", None, "ctx"),
        P("exp", "ctx", None),
        P(("exp", "ctx"), None),
        P(("exp", "ctx"), None),
    )
    return jax.shard_map(
        on_device, mesh=mesh, in_specs=placed, out_specs=P(("exp", "ctx"), None), check_vma=False
    )
```

```python
import functools

import jax
import jax.numpy as jnp
from jax import lax
from jax.experimental import pallas as pl
from jax.experimental.pallas import tpu as pltpu
from jax.sharding import PartitionSpec as P

D = 2880
QUERY_HEADS = 64
KEY_VALUE_HEADS = 8
HEAD_SIZE = 64
ALL_EXPERTS = 128
TOPK = 4
CAP = 8
TOK = 128
FFS = 360
NX = 4
QUARTER = ALL_EXPERTS // TOPK
WINDOW = 4
DOC_ROWS = 16
PACK_ROWS = TOK + DOC_ROWS
PACK_COLS = 1280
HALF = D // 2
MIB = 1024 * 1024

VMEM = pltpu.VMEM
ANY = pl.ANY
SMEM = pltpu.SMEM

RIGHT = [(4 * y + x, 4 * y + (x + 1) % 4) for y in range(2) for x in range(4)]
LEFT = [(4 * y + x, 4 * y + (x + 3) % 4) for y in range(2) for x in range(4)]
FLIP = [(c, c ^ 4) for c in range(8)]

NT = (((1,), (1,)), ((), ()))
TN = (((0,), (0,)), ((), ()))


def go_right(v):
    return lax.ppermute(v, "ctx", RIGHT)


def go_left(v):
    return lax.ppermute(v, "ctx", LEFT)


def go_flip(v):
    return lax.ppermute(v, "ctx", FLIP)


def params(mib):
    return pltpu.CompilerParams(vmem_limit_bytes=mib * MIB)


def spec(space):
    return pl.BlockSpec(memory_space=space)


def add(*pieces):
    total = pieces[0].astype(jnp.float32)
    for piece in pieces[1:]:
        total = total + piece.astype(jnp.float32)
    return total.astype(jnp.bfloat16)


def pack_kernel(q_ref, k_ref, v_ref, seg_ref, out_ref):
    lane = lax.broadcasted_iota(jnp.int32, (TOK, 128), 1)
    docs = jnp.broadcast_to(seg_ref[...].astype(jnp.float32), (DOC_ROWS, 128))
    eighth = jnp.asarray(0.125, jnp.bfloat16)
    for x in range(NX):
        out_ref[x, :TOK, 0:512] = q_ref[:, 512 * x : 512 * x + 512] * eighth
        out_ref[x, :TOK, 512:1024] = q_ref[:, 2048 + 512 * x : 2048 + 512 * x + 512] * eighth
        for ref, start in ((k_ref, 1024), (v_ref, 1152)):
            base = 128 * (x // 2)
            low = ref[:, base : base + 128].astype(jnp.float32)
            high = ref[:, 256 + base : 256 + base + 128].astype(jnp.float32)
            if x % 2 == 0:
                high = pltpu.roll(high, 64, 1)
            else:
                low = pltpu.roll(low, 64, 1)
            out_ref[x, :TOK, start : start + 128] = jnp.where(lane < 64, low, high).astype(
                jnp.bfloat16
            )
        out_ref[x, TOK:, 0:1024] = jnp.zeros((DOC_ROWS, 1024), jnp.bfloat16)
        out_ref[x, TOK:, 1024:1152] = docs.astype(jnp.bfloat16)
        out_ref[x, TOK:, 1152:1280] = jnp.zeros((DOC_ROWS, 128), jnp.bfloat16)


def pack(queries, keys, values, segments):
    return pl.pallas_call(
        pack_kernel,
        out_shape=jax.ShapeDtypeStruct((NX, PACK_ROWS, PACK_COLS), jnp.bfloat16),
        in_specs=[spec(VMEM)] * 4,
        out_specs=spec(VMEM),
        compiler_params=params(10),
        cost_estimate=pl.CostEstimate(flops=0, bytes_accessed=5 << 20, transcendentals=0),
    )(queries, keys, values, segments.reshape(1, TOK))


def attend_kernel(steps, sinks, pack_ref, low_ref, out_ref, key_a, key_b, val_a, val_b, doc_row, bias, hold):
    ctx = lax.axis_index("ctx")
    y, x = ctx // NX, lax.rem(ctx, NX)
    lane = lax.broadcasted_iota(jnp.int32, (TOK, 128), 1)

    def place(ref, b, first, slot):
        rows = pl.ds(pl.multiple_of(slot * TOK, TOK), TOK)
        keys = ref[b, 0:TOK, first : first + 128].astype(jnp.float32)
        vals = ref[b, 0:TOK, first + 128 : first + 256].astype(jnp.float32)
        for g in range(2):
            mine = (lane < 64) if g == 0 else (lane >= 64)
            k_here = jnp.where(mine, keys, 0.0)
            v_here = jnp.where(mine, vals, 1.0)
            k_roll = pltpu.roll(k_here, 64, 1)
            v_roll = pltpu.roll(v_here, 64, 1)
            pair_k = (k_here, k_roll) if g == 0 else (k_roll, k_here)
            pair_v = (v_here, v_roll) if g == 0 else (v_roll, v_here)
            key_a[g, rows] = pair_k[0].astype(jnp.bfloat16)
            key_b[g, rows] = pair_k[1].astype(jnp.bfloat16)
            val_a[g, rows] = pair_v[0].astype(jnp.bfloat16)
            val_b[g, rows] = pair_v[1].astype(jnp.bfloat16)
        doc_row[:, rows] = ref[b, TOK : TOK + 8, first : first + 128].astype(jnp.float32)

    for b in range(NX):
        place(pack_ref, b, 1024, 4 * y + b)

    @pl.when(y == 1)
    def _():
        for b in range(NX):
            place(low_ref, b, 0, b)

    two = 2 * TOK
    upper = lax.broadcasted_iota(jnp.int32, (two, 128), 0) < TOK
    first = lax.broadcasted_iota(jnp.int32, (two, 128), 1) < 64

    for index, step in enumerate(steps):
        j = lax.rem(x + step, NX)
        block = 4 * y + j
        own_docs = doc_row[0:1, pl.ds(pl.multiple_of(block * TOK, TOK), TOK)]
        query_docs = jnp.transpose(jnp.broadcast_to(own_docs, (TOK, TOK)))
        query_place = block * TOK + lax.broadcasted_iota(jnp.int32, (TOK, 128), 0)

        def run(chunks, index=index, j=j, query_docs=query_docs, query_place=query_place):
            for t in range(2 * chunks):
                cols = slice(128 * t, 128 * t + 128)
                allowed = (query_docs == doc_row[0:1, cols]) & (128 * t + lane <= query_place)
                bias[:, cols] = jnp.where(allowed, 0.0, -jnp.inf)

            def quad(p, carry):
                g = p // 2
                base = pl.multiple_of(p * 256, 256)
                place_out = pl.multiple_of(512 * lax.rem(g + y, 2) + 256 * lax.rem(p, 2), 256)
                q = jnp.concatenate(
                    [
                        pack_ref[j, 0:TOK, pl.ds(base, 128)],
                        pack_ref[j, 0:TOK, pl.ds(pl.multiple_of(base + 128, 128), 128)],
                    ],
                    axis=0,
                )
                head = 8 * x + 32 * g + 4 * lax.rem(p, 2)
                tops, sink_rows = [], []
                for which, key_ref in enumerate((key_a, key_b)):
                    sink = jnp.where(upper, sinks[head + which], sinks[head + 2 + which])
                    top = sink
                    for c in range(chunks):
                        cols = slice(256 * c, 256 * c + 256)
                        s = lax.dot_general(
                            q, key_ref[g, cols], NT, preferred_element_type=jnp.float32
                        )
                        mask = bias[:, cols]
                        s = s + jnp.concatenate([mask, mask], axis=0)
                        hold[which, :, cols] = s
                        top = jnp.maximum(top, jnp.maximum(s[:, 0:128], s[:, 128:256]))
                    tops.append(jnp.max(top, axis=1, keepdims=True))
                    sink_rows.append(sink)
                outs = []
                for which, val_ref in enumerate((val_a, val_b)):
                    total = jnp.zeros((two, 128), jnp.float32)
                    for c in range(chunks):
                        cols = slice(256 * c, 256 * c + 256)
                        prob = jnp.exp(hold[which, :, cols] - tops[which]).astype(jnp.bfloat16)
                        total = total + jnp.dot(
                            prob, val_ref[g, cols], preferred_element_type=jnp.float32
                        )
                    outs.append(total)
                numer = jnp.where(first, outs[0], outs[1])
                divisor = pltpu.roll(jnp.where(first, outs[1], outs[0]), 64, 1)
                gap = jnp.where(first, sink_rows[0] - tops[0], sink_rows[1] - tops[1])
                result = (numer / (divisor + jnp.exp(gap))).astype(jnp.bfloat16)
                rows = slice(index * TOK, index * TOK + TOK)
                out_ref[rows, pl.ds(place_out, 128)] = result[0:TOK]
                out_ref[rows, pl.ds(pl.multiple_of(place_out + 128, 128), 128)] = result[TOK:]
                return carry

            lax.fori_loop(0, 4, quad, 0)

        for quarter in range(4):

            @pl.when(block // 2 == quarter)
            def _(run=run, quarter=quarter):
                run(quarter + 1)


def attend(steps, sinks, packed, low):
    return pl.pallas_call(
        functools.partial(attend_kernel, steps),
        out_shape=jax.ShapeDtypeStruct((len(steps) * TOK, 1024), jnp.bfloat16),
        in_specs=[spec(SMEM), spec(VMEM), spec(VMEM)],
        out_specs=spec(VMEM),
        scratch_shapes=[
            pltpu.VMEM((2, 1024, 128), jnp.bfloat16),
            pltpu.VMEM((2, 1024, 128), jnp.bfloat16),
            pltpu.VMEM((2, 1024, 128), jnp.bfloat16),
            pltpu.VMEM((2, 1024, 128), jnp.bfloat16),
            pltpu.VMEM((8, 1024), jnp.float32),
            pltpu.VMEM((TOK, 1024), jnp.float32),
            pltpu.VMEM((2, 2 * TOK, 1024), jnp.float32),
        ],
        compiler_params=params(14),
        cost_estimate=pl.CostEstimate(
            flops=2 << 30, bytes_accessed=4 << 20, transcendentals=0
        ),
    )(sinks, packed, low)


def project_kernel(sides, attn, w_own, w_first, w_second, *refs):
    core = lax.rem(lax.axis_index("exp"), 2)
    if sides:
        from_left, from_right, next_a, next_b, prev_a, prev_b = refs
    else:
        out_a, out_b = refs
    for part, (w_near, base) in enumerate(((w_first, core * HALF), (w_second, (1 - core) * HALF))):
        for start in range(0, HALF, 288):
            near = slice(start, start + 288)
            rows = pl.ds(pl.multiple_of(base + start, 16), 288)
            total = lax.dot_general(
                w_own[rows], attn[:, 0:512], NT, preferred_element_type=jnp.float32
            ) + lax.dot_general(
                w_near[near], attn[:, 512:1024], NT, preferred_element_type=jnp.float32
            )
            if not sides:
                (out_a, out_b)[part][near] = total.astype(jnp.bfloat16)
                continue
            after, before = total[:, 0:128], total[:, 128:256]
            if part == 0:
                after = after + from_left[near].astype(jnp.float32)
            else:
                before = before + from_right[near].astype(jnp.float32)
            (next_a, next_b)[part][near] = after.astype(jnp.bfloat16)
            (prev_a, prev_b)[part][near] = before.astype(jnp.bfloat16)


def project(attn, w_own, w_first, w_second, *extra):
    sides = len(extra) > 0
    count = 4 if sides else 2
    return pl.pallas_call(
        functools.partial(project_kernel, sides),
        out_shape=(jax.ShapeDtypeStruct((HALF, TOK), jnp.bfloat16),) * count,
        in_specs=[spec(VMEM)] * (4 + len(extra)),
        out_specs=(spec(VMEM),) * count,
        compiler_params=params(10),
        cost_estimate=pl.CostEstimate(flops=3 << 29, bytes_accessed=4 << 20, transcendentals=0),
    )(attn, w_own, w_first, w_second, *extra)


def slot_table(ids):
    local = ids % QUARTER
    chosen = jnp.where(local < WINDOW, ids // QUARTER * WINDOW + local, -1)
    slot = lax.broadcasted_iota(jnp.int32, (TOK, TOK), 0)
    expert = slot // CAP
    hits = [chosen[k : k + 1] == expert for k in range(TOPK)]
    named = functools.reduce(jnp.logical_or, hits)
    before = lax.broadcasted_iota(jnp.int32, (TOK, TOK), 0) < lax.broadcasted_iota(
        jnp.int32, (TOK, TOK), 1
    )
    rank = jnp.dot(
        jnp.where(named, 1.0, 0.0).astype(jnp.bfloat16),
        jnp.where(before, 1.0, 0.0).astype(jnp.bfloat16),
        preferred_element_type=jnp.float32,
    )
    table = named & (rank == (slot % CAP).astype(jnp.float32))
    return table, hits


def norm_kernel(
    resid, own_a, own_b, left_a, left_b, right_a, right_b, gain, ids, hidden_ref, send_ref, gain_row
):
    core = lax.rem(lax.axis_index("exp"), 2)
    gain_row[...] = jnp.ones_like(gain_row)
    gain_row[:, 0:D] = gain[...]
    square = jnp.zeros((8, TOK), jnp.float32)
    for base, own, left, right in (
        (core * HALF, own_a, left_a, right_a),
        ((1 - core) * HALF, own_b, left_b, right_b),
    ):
        for start in range(0, HALF, 160):
            near = slice(start, start + 160)
            rows = pl.ds(pl.multiple_of(base + start, 16), 160)
            total = own[near].astype(jnp.float32)
            total = total + left[near].astype(jnp.float32) + right[near].astype(jnp.float32)
            hidden = resid[rows].astype(jnp.float32) + total
            hidden_ref[rows] = hidden
            square = square + jnp.sum((hidden * hidden).reshape(20, 8, TOK), axis=0)
    mean = jnp.sum(square, axis=0, keepdims=True) * (1.0 / D)
    scale = lax.rsqrt(mean + 1e-05)
    table, _ = slot_table(ids[...])
    table = jnp.where(table, 1.0, 0.0).astype(jnp.bfloat16)
    for start in range(0, D, 128):
        size = min(128, D - start)
        rows = slice(start, start + size)
        gains = jnp.transpose(jnp.broadcast_to(gain_row[:, start : start + 128], (128, 128)))
        normed = (hidden_ref[rows] * scale * gains[0:size]).astype(jnp.bfloat16)
        send_ref[:, rows] = lax.dot_general(
            table, normed, NT, preferred_element_type=jnp.float32
        ).astype(jnp.bfloat16)


def norm(resid, own_a, own_b, left_a, left_b, right_a, right_b, gain, ids):
    return pl.pallas_call(
        norm_kernel,
        out_shape=(
            jax.ShapeDtypeStruct((D, TOK), jnp.float32),
            jax.ShapeDtypeStruct((TOK, D), jnp.bfloat16),
        ),
        in_specs=[spec(VMEM)] * 9,
        out_specs=(spec(VMEM), spec(VMEM)),
        scratch_shapes=[pltpu.VMEM((1, D + 64), jnp.float32)],
        compiler_params=params(10),
        cost_estimate=pl.CostEstimate(flops=1 << 27, bytes_accessed=6 << 20, transcendentals=0),
    )(resid, own_a, own_b, left_a, left_b, right_a, right_b, gain, ids)


def combine_kernel(hidden, back, ids, weights, out_ref):
    table, hits = slot_table(ids[...])
    chosen_weight = jnp.zeros((TOK, TOK), jnp.float32)
    for k in range(TOPK):
        chosen_weight = chosen_weight + jnp.where(hits[k], weights[k : k + 1], 0.0)
    share = jnp.where(table, chosen_weight, 0.0)
    high = share.astype(jnp.bfloat16)
    low = (share - high.astype(jnp.float32)).astype(jnp.bfloat16)
    for start in range(0, D, 128):
        cols = slice(start, min(start + 128, D))
        rows = back[:, cols]
        moe = lax.dot_general(rows, high, TN, preferred_element_type=jnp.float32)
        moe = moe + lax.dot_general(rows, low, TN, preferred_element_type=jnp.float32)
        out_ref[cols] = (hidden[cols] + moe).astype(jnp.bfloat16)


def combine(hidden, back, ids, weights):
    return pl.pallas_call(
        combine_kernel,
        out_shape=jax.ShapeDtypeStruct((D, TOK), jnp.bfloat16),
        in_specs=[spec(VMEM)] * 4,
        out_specs=spec(VMEM),
        compiler_params=params(10),
        cost_estimate=pl.CostEstimate(flops=1 << 28, bytes_accessed=3 << 20, transcendentals=0),
    )(hidden, back, ids, weights)


PAIR_DOWN, PAIR_ROWS = 368, 728


def pair_kernel(up, down, out):
    out[0:FFS] = up[...]
    out[FFS:PAIR_DOWN] = jnp.zeros((PAIR_DOWN - FFS, D), jnp.bfloat16)
    out[PAIR_DOWN:PAIR_ROWS] = down[...]


def pair(up, down):
    return pl.pallas_call(
        pair_kernel,
        out_shape=jax.ShapeDtypeStruct((PAIR_ROWS, D), jnp.bfloat16),
        in_specs=[spec(VMEM)] * 2,
        out_specs=spec(VMEM),
        compiler_params=params(10),
        cost_estimate=pl.CostEstimate(flops=0, bytes_accessed=8 << 20, transcendentals=0),
    )(up, down)


def expert_kernel(sizes, *refs):
    count = len(sizes)
    pieces, weights, outs = refs[:count], refs[count : count + 7], refs[count + 7 : 2 * count + 7]
    rows_x, gate_near, up_near, down_near, sem = refs[2 * count + 7 :]
    gate_own, up_own, down_own, gate_0, gate_1, pair_0, pair_1 = weights
    core = lax.rem(lax.axis_index("exp"), 2)
    up_rows, down_rows = pl.ds(0, FFS), pl.ds(PAIR_DOWN, FFS)
    near = (
        ((gate_0, gate_1), gate_near),
        ((pair_0.at[up_rows], pair_1.at[up_rows]), up_near),
        ((pair_0.at[down_rows], pair_1.at[down_rows]), down_near),
    )

    def by_core(index, act):
        sources, held = near[index]
        for which, source in enumerate(sources):

            @pl.when(core == which)
            def _(source=source):
                act(pltpu.make_async_copy(source, held, sem.at[count + index]))

    copies = []
    start = 0
    for index, (piece, size) in enumerate(zip(pieces, sizes)):
        copies.append(
            pltpu.make_async_copy(piece, rows_x.at[pl.ds(start, size)], sem.at[index])
        )
        start += size
    for copy in copies:
        copy.start()
    for index in range(3):
        by_core(index, lambda copy: copy.start())
    for copy in copies:
        copy.wait()
    x = rows_x[...]

    def hidden_units(gate, up, ready):
        g = lax.dot_general(x, gate[...], NT, preferred_element_type=jnp.float32)
        ready()
        v = lax.dot_general(x, up[...], NT, preferred_element_type=jnp.float32)
        return ((v + 1.0) * g * jax.nn.sigmoid(1.702 * g)).astype(jnp.bfloat16)

    act_own = hidden_units(gate_own, up_own, lambda: None)
    by_core(0, lambda copy: copy.wait())
    act_near = hidden_units(gate_near, up_near, lambda: by_core(1, lambda copy: copy.wait()))
    by_core(2, lambda copy: copy.wait())
    for first in range(0, D, 512):
        cols = slice(first, min(first + 512, D))
        part = jnp.dot(act_own, down_own[:, cols], preferred_element_type=jnp.float32)
        part = part + jnp.dot(act_near, down_near[:, cols], preferred_element_type=jnp.float32)
        part = part.astype(jnp.bfloat16)
        start = 0
        for out, size in zip(outs, sizes):
            out[:, cols] = part[start : start + size]
            start += size


def experts(pieces, weights):
    sizes = tuple(piece.shape[0] for piece in pieces)
    total = sum(sizes)
    return pl.pallas_call(
        functools.partial(expert_kernel, sizes),
        out_shape=tuple(jax.ShapeDtypeStruct((size, D), jnp.bfloat16) for size in sizes),
        in_specs=[spec(ANY)] * len(sizes) + [spec(VMEM)] * 3 + [spec(ANY)] * 4,
        out_specs=tuple(spec(VMEM) for _ in sizes),
        scratch_shapes=[pltpu.VMEM((total, D), jnp.bfloat16)]
        + [pltpu.VMEM((FFS, D), jnp.bfloat16)] * 3
        + [pltpu.SemaphoreType.DMA((len(sizes) + 3,))],
        compiler_params=params(18),
        cost_estimate=pl.CostEstimate(
            flops=12 * total * D * FFS, bytes_accessed=8 << 20, transcendentals=0
        ),
    )(*pieces, *weights)


def over_all(move):
    pairs = []
    for c in range(8):
        for e in range(16):
            y, x, z, hi, core = move(c // 4, c % 4, e // 4, e // 2 % 2, e % 2)
            pairs.append((c * 16 + e, (y * 4 + x) * 16 + z * 4 + hi * 2 + core))
    return pairs


def partner(y, x, z, hi, core):
    return (1 - y, x, z, hi, core) if core == 0 else (y, x ^ 1, z, hi, core)


def onward(y, x, z, hi, core):
    if core == 0:
        return y, (x + 1) % 4, z, hi, core
    across = x < 2 if y == 0 else x >= 2
    return (y, 3 - x, z, hi, core) if across else (1 - y, x, z, hi, core)


def across_y(y, x, z, hi, core):
    place = (2 * hi + y + (1 if y == 1 else 3)) % 4
    return place % 2, x, z, place // 2, core


def permute(v, pairs):
    return lax.ppermute(v, ("ctx", "exp"), pairs)


NEXT = over_all(onward)
BACK = [(b, a) for a, b in NEXT]
PARTNER = over_all(partner)
PARTNER_0 = [(a, b if a % 2 == 0 else a) for a, b in PARTNER]
PARTNER_1 = [(a, b if a % 2 == 1 else a) for a, b in PARTNER]
ACROSS = over_all(across_y)
SWAP = over_all(lambda y, x, z, hi, core: (y, x, z, hi, 1 - core))


def exchange_experts(arrived, weights):
    half = TOK // 2
    own_a, own_b = arrived[:half], arrived[half:]
    prev_a, next_b = permute(own_a, NEXT), permute(own_b, BACK)
    prev_b, next_a = permute(own_b, NEXT), permute(own_a, BACK)
    opp_a, opp_b = permute(prev_a, NEXT), permute(next_b, BACK)
    oo_a, oo_b, op_a, on_b = experts((own_a, own_b, prev_a, next_b), weights)
    got_b, got_a = permute(on_b, NEXT), permute(op_a, BACK)
    opp_a, opp_b, prev_b, next_a, oo_a, oo_b = lax.optimization_barrier(
        (opp_a, opp_b, prev_b, next_a, oo_a, oo_b)
    )
    far_a, far_b, op_b, on_a = experts((opp_a, opp_b, prev_b, next_a), weights)
    got_a, got_b, far_a, far_b, op_b, on_a = lax.optimization_barrier(
        (got_a, got_b, far_a, far_b, op_b, on_a)
    )
    more_a = permute(add(on_a, permute(far_a, NEXT)), NEXT)
    more_b = permute(add(op_b, permute(far_b, BACK)), BACK)
    return jnp.concatenate([add(oo_a, got_a, more_a), add(oo_b, got_b, more_b)], axis=0)


def on_device(
    resid_in,
    queries,
    keys,
    values,
    sinks,
    segments,
    norm_gain,
    out_weight,
    gate_weight,
    up_weight,
    down_weight,
    expert_ids,
    route_weights,
):
    core = lax.axis_index("exp") % 2
    gate, up, down = gate_weight[0].T, up_weight[0].T, down_weight[0]
    w_own = out_weight.T

    mine = lax.dynamic_slice_in_dim(w_own, core * HALF, HALF, 0)
    mine, gate_out = lax.optimization_barrier((mine, gate))
    w_first = permute(mine, ACROSS)
    gate_0 = permute(gate_out, PARTNER_0)

    packed = pack(queries, keys, values, segments)
    packed = lax.all_to_all(
        packed,
        "ctx",
        split_axis=0,
        concat_axis=0,
        tiled=True,
        axis_index_groups=[[0, 1, 2, 3], [4, 5, 6, 7]],
    )
    packed, gate_0, gate_out = lax.optimization_barrier((packed, gate_0, gate))
    low = lax.ppermute(packed[:, :, 1024:], "ctx", [(x, x + 4) for x in range(4)])
    gate_1 = permute(gate_out, PARTNER_1)
    both = pair(up, down)
    low, w_first, both = lax.optimization_barrier((low, w_first, both))
    w_second = permute(w_first, SWAP)
    pair_0 = permute(both, PARTNER_0)

    weights = (w_own, w_first, w_second)
    opp_a, opp_b = project(attend((2,), sinks, packed, low), *weights)
    opp_a, opp_b, packed, low = lax.optimization_barrier((opp_a, opp_b, packed, low))
    from_left, from_right = go_right(opp_a), go_left(opp_b)
    attn = attend((1, 3), sinks, packed, low)
    attn, gate_1 = lax.optimization_barrier((attn, gate_1))
    next_a, next_b, prev_a, prev_b = project(attn, *weights, from_left, from_right)
    next_a, next_b, prev_a, prev_b, packed, low = lax.optimization_barrier(
        (next_a, next_b, prev_a, prev_b, packed, low)
    )
    right_b, left_a = go_right(next_b), go_left(prev_a)
    right_a, left_b = go_right(next_a), go_left(prev_b)
    attn = attend((0,), sinks, packed, low)
    own_a, own_b = project(attn, *weights)
    right_a, right_b, left_a, left_b, own_a, own_b, both = lax.optimization_barrier(
        (right_a, right_b, left_a, left_b, own_a, own_b, both)
    )
    pair_1 = permute(both, PARTNER_1)

    ids = expert_ids.T
    hidden, send = norm(
        resid_in.T, own_a, own_b, right_a, right_b, left_a, left_b, norm_gain.reshape(1, D), ids
    )
    send, pair_0 = lax.optimization_barrier((send, pair_0))
    arrived = lax.all_to_all(send, "exp", split_axis=0, concat_axis=0, tiled=True)
    summed = exchange_experts(arrived, (gate, up, down, gate_0, gate_1, pair_0, pair_1))
    back = lax.all_to_all(summed, "exp", split_axis=0, concat_axis=0, tiled=True)
    return combine(hidden, back, ids, route_weights.T).T


def solution(mesh):
    placed = (
        P(("exp", "ctx"), None),
        P(("exp", "ctx"), None),
        P(("exp", "ctx"), None),
        P(("exp", "ctx"), None),
        P(),
        P(("exp", "ctx")),
        P(),
        P("ctx", None),
        P("exp", None, "ctx"),
        P("exp", None, "ctx"),
        P("exp", "ctx", None),
        P(("exp", "ctx"), None),
        P(("exp", "ctx"), None),
    )
    return jax.shard_map(
        on_device, mesh=mesh, in_specs=placed, out_specs=P(("exp", "ctx"), None), check_vma=False
    )
```

```python
import functools

import jax
import jax.numpy as jnp
from jax import lax
from jax.experimental import pallas as pl
from jax.experimental.pallas import tpu as pltpu
from jax.sharding import PartitionSpec as P

D = 2880
QUERY_HEADS = 64
KEY_VALUE_HEADS = 8
HEAD_SIZE = 64
ALL_EXPERTS = 128
TOPK = 4
CAP = 8
TOK = 128
FFS = 360
NX = 4
QUARTER = ALL_EXPERTS // TOPK
WINDOW = 4
DOC_ROWS = 16
PACK_ROWS = TOK + DOC_ROWS
PACK_COLS = 1280
HALF = D // 2
MIB = 1024 * 1024

VMEM = pltpu.VMEM
ANY = pl.ANY
SMEM = pltpu.SMEM

RIGHT = [(4 * y + x, 4 * y + (x + 1) % 4) for y in range(2) for x in range(4)]
LEFT = [(4 * y + x, 4 * y + (x + 3) % 4) for y in range(2) for x in range(4)]
FLIP = [(c, c ^ 4) for c in range(8)]

NT = (((1,), (1,)), ((), ()))
TN = (((0,), (0,)), ((), ()))


def go_right(v):
    return lax.ppermute(v, "ctx", RIGHT)


def go_left(v):
    return lax.ppermute(v, "ctx", LEFT)


def go_flip(v):
    return lax.ppermute(v, "ctx", FLIP)


def params(mib):
    return pltpu.CompilerParams(vmem_limit_bytes=mib * MIB)


def spec(space):
    return pl.BlockSpec(memory_space=space)


def add(*pieces):
    total = pieces[0].astype(jnp.float32)
    for piece in pieces[1:]:
        total = total + piece.astype(jnp.float32)
    return total.astype(jnp.bfloat16)


def pack_kernel(q_ref, k_ref, v_ref, seg_ref, out_ref):
    lane = lax.broadcasted_iota(jnp.int32, (TOK, 128), 1)
    docs = jnp.broadcast_to(seg_ref[...].astype(jnp.float32), (DOC_ROWS, 128))
    eighth = jnp.asarray(0.125, jnp.bfloat16)
    for x in range(NX):
        out_ref[x, :TOK, 0:512] = q_ref[:, 512 * x : 512 * x + 512] * eighth
        out_ref[x, :TOK, 512:1024] = q_ref[:, 2048 + 512 * x : 2048 + 512 * x + 512] * eighth
        for ref, start in ((k_ref, 1024), (v_ref, 1152)):
            base = 128 * (x // 2)
            low = ref[:, base : base + 128].astype(jnp.float32)
            high = ref[:, 256 + base : 256 + base + 128].astype(jnp.float32)
            if x % 2 == 0:
                high = pltpu.roll(high, 64, 1)
            else:
                low = pltpu.roll(low, 64, 1)
            out_ref[x, :TOK, start : start + 128] = jnp.where(lane < 64, low, high).astype(
                jnp.bfloat16
            )
        out_ref[x, TOK:, 0:1024] = jnp.zeros((DOC_ROWS, 1024), jnp.bfloat16)
        out_ref[x, TOK:, 1024:1152] = docs.astype(jnp.bfloat16)
        out_ref[x, TOK:, 1152:1280] = jnp.zeros((DOC_ROWS, 128), jnp.bfloat16)


def pack(queries, keys, values, segments):
    return pl.pallas_call(
        pack_kernel,
        out_shape=jax.ShapeDtypeStruct((NX, PACK_ROWS, PACK_COLS), jnp.bfloat16),
        in_specs=[spec(VMEM)] * 4,
        out_specs=spec(VMEM),
        compiler_params=params(10),
        cost_estimate=pl.CostEstimate(flops=0, bytes_accessed=5 << 20, transcendentals=0),
    )(queries, keys, values, segments.reshape(1, TOK))


def attend_kernel(steps, sinks, pack_ref, low_ref, out_ref, key_a, key_b, val_a, val_b, doc_row, bias, hold):
    ctx = lax.axis_index("ctx")
    y, x = ctx // NX, lax.rem(ctx, NX)
    lane = lax.broadcasted_iota(jnp.int32, (TOK, 128), 1)

    def place(ref, b, first, slot):
        rows = pl.ds(pl.multiple_of(slot * TOK, TOK), TOK)
        keys = ref[b, 0:TOK, first : first + 128].astype(jnp.float32)
        vals = ref[b, 0:TOK, first + 128 : first + 256].astype(jnp.float32)
        for g in range(2):
            mine = (lane < 64) if g == 0 else (lane >= 64)
            k_here = jnp.where(mine, keys, 0.0)
            v_here = jnp.where(mine, vals, 1.0)
            k_roll = pltpu.roll(k_here, 64, 1)
            v_roll = pltpu.roll(v_here, 64, 1)
            pair_k = (k_here, k_roll) if g == 0 else (k_roll, k_here)
            pair_v = (v_here, v_roll) if g == 0 else (v_roll, v_here)
            key_a[g, rows] = pair_k[0].astype(jnp.bfloat16)
            key_b[g, rows] = pair_k[1].astype(jnp.bfloat16)
            val_a[g, rows] = pair_v[0].astype(jnp.bfloat16)
            val_b[g, rows] = pair_v[1].astype(jnp.bfloat16)
        doc_row[:, rows] = ref[b, TOK : TOK + 8, first : first + 128].astype(jnp.float32)

    for b in range(NX):
        place(pack_ref, b, 1024, 4 * y + b)

    @pl.when(y == 1)
    def _():
        for b in range(NX):
            place(low_ref, b, 0, b)

    two = 2 * TOK
    upper = lax.broadcasted_iota(jnp.int32, (two, 128), 0) < TOK
    first = lax.broadcasted_iota(jnp.int32, (two, 128), 1) < 64

    def block_rows(index, carry):
        j = lax.rem(x + steps[0] + index * (steps[-1] - steps[0]), NX)
        block = 4 * y + j
        own_docs = doc_row[0:1, pl.ds(pl.multiple_of(block * TOK, TOK), TOK)]
        query_docs = jnp.transpose(jnp.broadcast_to(own_docs, (TOK, TOK)))
        query_place = block * TOK + lax.broadcasted_iota(jnp.int32, (TOK, 128), 0)

        def run(chunks):
            for t in range(2 * chunks):
                cols = slice(128 * t, 128 * t + 128)
                allowed = (query_docs == doc_row[0:1, cols]) & (128 * t + lane <= query_place)
                bias[:, cols] = jnp.where(allowed, 0.0, -jnp.inf)

            def quad(p, carry):
                g = p // 2
                base = pl.multiple_of(p * 256, 256)
                place_out = pl.multiple_of(512 * lax.rem(g + y, 2) + 256 * lax.rem(p, 2), 256)
                q = jnp.concatenate(
                    [
                        pack_ref[j, 0:TOK, pl.ds(base, 128)],
                        pack_ref[j, 0:TOK, pl.ds(pl.multiple_of(base + 128, 128), 128)],
                    ],
                    axis=0,
                )
                head = 8 * x + 32 * g + 4 * lax.rem(p, 2)
                tops, sink_rows = [], []
                for which, key_ref in enumerate((key_a, key_b)):
                    sink = jnp.where(upper, sinks[head + which], sinks[head + 2 + which])
                    top = sink
                    for c in range(chunks):
                        cols = slice(256 * c, 256 * c + 256)
                        s = lax.dot_general(
                            q, key_ref[g, cols], NT, preferred_element_type=jnp.float32
                        )
                        mask = bias[:, cols]
                        s = s + jnp.concatenate([mask, mask], axis=0)
                        hold[which, :, cols] = s
                        top = jnp.maximum(top, jnp.maximum(s[:, 0:128], s[:, 128:256]))
                    tops.append(jnp.max(top, axis=1, keepdims=True))
                    sink_rows.append(sink)
                outs = []
                for which, val_ref in enumerate((val_a, val_b)):
                    total = jnp.zeros((two, 128), jnp.float32)
                    for c in range(chunks):
                        cols = slice(256 * c, 256 * c + 256)
                        prob = jnp.exp(hold[which, :, cols] - tops[which]).astype(jnp.bfloat16)
                        total = total + jnp.dot(
                            prob, val_ref[g, cols], preferred_element_type=jnp.float32
                        )
                    outs.append(total)
                numer = jnp.where(first, outs[0], outs[1])
                divisor = pltpu.roll(jnp.where(first, outs[1], outs[0]), 64, 1)
                gap = jnp.where(first, sink_rows[0] - tops[0], sink_rows[1] - tops[1])
                result = (numer / (divisor + jnp.exp(gap))).astype(jnp.bfloat16)
                rows = pl.ds(pl.multiple_of(index * TOK, TOK), TOK)
                out_ref[rows, pl.ds(place_out, 128)] = result[0:TOK]
                out_ref[rows, pl.ds(pl.multiple_of(place_out + 128, 128), 128)] = result[TOK:]
                return carry

            lax.fori_loop(0, 4, quad, 0)

        for quarter in range(4):

            @pl.when(block // 2 == quarter)
            def _(quarter=quarter):
                run(quarter + 1)

        return carry

    lax.fori_loop(0, len(steps), block_rows, 0)


def attend(steps, sinks, packed, low):
    return pl.pallas_call(
        functools.partial(attend_kernel, steps),
        out_shape=jax.ShapeDtypeStruct((len(steps) * TOK, 1024), jnp.bfloat16),
        in_specs=[spec(SMEM), spec(VMEM), spec(VMEM)],
        out_specs=spec(VMEM),
        scratch_shapes=[
            pltpu.VMEM((2, 1024, 128), jnp.bfloat16),
            pltpu.VMEM((2, 1024, 128), jnp.bfloat16),
            pltpu.VMEM((2, 1024, 128), jnp.bfloat16),
            pltpu.VMEM((2, 1024, 128), jnp.bfloat16),
            pltpu.VMEM((8, 1024), jnp.float32),
            pltpu.VMEM((TOK, 1024), jnp.float32),
            pltpu.VMEM((2, 2 * TOK, 1024), jnp.float32),
        ],
        compiler_params=params(14),
        cost_estimate=pl.CostEstimate(
            flops=2 << 30, bytes_accessed=4 << 20, transcendentals=0
        ),
    )(sinks, packed, low)


def project_kernel(sides, attn, w_own, w_first, w_second, *refs):
    core = lax.rem(lax.axis_index("exp"), 2)
    if sides:
        from_left, from_right, to_right, to_left = refs
    else:
        out_a, out_b = refs
    for part, (w_near, base) in enumerate(((w_first, core * HALF), (w_second, (1 - core) * HALF))):
        for start in range(0, HALF, 288):
            near = slice(start, start + 288)
            rows = pl.ds(pl.multiple_of(base + start, 16), 288)
            total = lax.dot_general(
                w_own[rows], attn[:, 0:512], NT, preferred_element_type=jnp.float32
            ) + lax.dot_general(
                w_near[near], attn[:, 512:1024], NT, preferred_element_type=jnp.float32
            )
            if not sides:
                (out_a, out_b)[part][near] = total.astype(jnp.bfloat16)
                continue
            after, before = total[:, 0:128], total[:, 128:256]
            if part == 0:
                after = after + from_left[near].astype(jnp.float32)
            else:
                before = before + from_right[near].astype(jnp.float32)
            to_right[rows] = after.astype(jnp.bfloat16)
            to_left[rows] = before.astype(jnp.bfloat16)


def project(attn, w_own, w_first, w_second, *extra):
    sides = len(extra) > 0
    rows = D if sides else HALF
    return pl.pallas_call(
        functools.partial(project_kernel, sides),
        out_shape=(jax.ShapeDtypeStruct((rows, TOK), jnp.bfloat16),) * 2,
        in_specs=[spec(VMEM)] * (4 + len(extra)),
        out_specs=(spec(VMEM),) * 2,
        compiler_params=params(10),
        cost_estimate=pl.CostEstimate(flops=3 << 29, bytes_accessed=4 << 20, transcendentals=0),
    )(attn, w_own, w_first, w_second, *extra)


def slot_table(ids):
    local = ids % QUARTER
    chosen = jnp.where(local < WINDOW, ids // QUARTER * WINDOW + local, -1)
    slot = lax.broadcasted_iota(jnp.int32, (TOK, TOK), 0)
    expert = slot // CAP
    hits = [chosen[k : k + 1] == expert for k in range(TOPK)]
    named = functools.reduce(jnp.logical_or, hits)
    before = lax.broadcasted_iota(jnp.int32, (TOK, TOK), 0) < lax.broadcasted_iota(
        jnp.int32, (TOK, TOK), 1
    )
    rank = jnp.dot(
        jnp.where(named, 1.0, 0.0).astype(jnp.bfloat16),
        jnp.where(before, 1.0, 0.0).astype(jnp.bfloat16),
        preferred_element_type=jnp.float32,
    )
    table = named & (rank == (slot % CAP).astype(jnp.float32))
    return table, hits


def norm_kernel(resid, own_a, own_b, left, right, gain, ids, hidden_ref, send_ref, gain_row):
    core = lax.rem(lax.axis_index("exp"), 2)
    gain_row[...] = jnp.ones_like(gain_row)
    gain_row[:, 0:D] = gain[...]
    square = jnp.zeros((8, TOK), jnp.float32)
    for base, own in ((core * HALF, own_a), ((1 - core) * HALF, own_b)):
        for start in range(0, HALF, 160):
            rows = pl.ds(pl.multiple_of(base + start, 16), 160)
            total = own[start : start + 160].astype(jnp.float32)
            total = total + left[rows].astype(jnp.float32) + right[rows].astype(jnp.float32)
            hidden = resid[rows].astype(jnp.float32) + total
            hidden_ref[rows] = hidden
            square = square + jnp.sum((hidden * hidden).reshape(20, 8, TOK), axis=0)
    mean = jnp.sum(square, axis=0, keepdims=True) * (1.0 / D)
    scale = lax.rsqrt(mean + 1e-05)
    table, _ = slot_table(ids[...])
    table = jnp.where(table, 1.0, 0.0).astype(jnp.bfloat16)
    for start in range(0, D, 128):
        size = min(128, D - start)
        rows = slice(start, start + size)
        gains = jnp.transpose(jnp.broadcast_to(gain_row[:, start : start + 128], (128, 128)))
        normed = (hidden_ref[rows] * scale * gains[0:size]).astype(jnp.bfloat16)
        send_ref[:, rows] = lax.dot_general(
            table, normed, NT, preferred_element_type=jnp.float32
        ).astype(jnp.bfloat16)


def norm(resid, own_a, own_b, left, right, gain, ids):
    return pl.pallas_call(
        norm_kernel,
        out_shape=(
            jax.ShapeDtypeStruct((D, TOK), jnp.float32),
            jax.ShapeDtypeStruct((TOK, D), jnp.bfloat16),
        ),
        in_specs=[spec(VMEM)] * 7,
        out_specs=(spec(VMEM), spec(VMEM)),
        scratch_shapes=[pltpu.VMEM((1, D + 64), jnp.float32)],
        compiler_params=params(10),
        cost_estimate=pl.CostEstimate(flops=1 << 27, bytes_accessed=6 << 20, transcendentals=0),
    )(resid, own_a, own_b, left, right, gain, ids)


def combine_kernel(hidden, back, ids, weights, out_ref):
    table, hits = slot_table(ids[...])
    chosen_weight = jnp.zeros((TOK, TOK), jnp.float32)
    for k in range(TOPK):
        chosen_weight = chosen_weight + jnp.where(hits[k], weights[k : k + 1], 0.0)
    share = jnp.where(table, chosen_weight, 0.0)
    high = share.astype(jnp.bfloat16)
    low = (share - high.astype(jnp.float32)).astype(jnp.bfloat16)
    for start in range(0, D, 128):
        cols = slice(start, min(start + 128, D))
        rows = back[:, cols]
        moe = lax.dot_general(rows, high, TN, preferred_element_type=jnp.float32)
        moe = moe + lax.dot_general(rows, low, TN, preferred_element_type=jnp.float32)
        out_ref[cols] = (hidden[cols] + moe).astype(jnp.bfloat16)


def combine(hidden, back, ids, weights):
    return pl.pallas_call(
        combine_kernel,
        out_shape=jax.ShapeDtypeStruct((D, TOK), jnp.bfloat16),
        in_specs=[spec(VMEM)] * 4,
        out_specs=spec(VMEM),
        compiler_params=params(10),
        cost_estimate=pl.CostEstimate(flops=1 << 28, bytes_accessed=3 << 20, transcendentals=0),
    )(hidden, back, ids, weights)


PAIR_DOWN, PAIR_ROWS = 368, 728


def pair_kernel(up, down, out):
    out[0:FFS] = up[...]
    out[FFS:PAIR_DOWN] = jnp.zeros((PAIR_DOWN - FFS, D), jnp.bfloat16)
    out[PAIR_DOWN:PAIR_ROWS] = down[...]


def pair(up, down):
    return pl.pallas_call(
        pair_kernel,
        out_shape=jax.ShapeDtypeStruct((PAIR_ROWS, D), jnp.bfloat16),
        in_specs=[spec(VMEM)] * 2,
        out_specs=spec(VMEM),
        compiler_params=params(10),
        cost_estimate=pl.CostEstimate(flops=0, bytes_accessed=8 << 20, transcendentals=0),
    )(up, down)


def expert_kernel(sizes, near, *refs):
    count = len(sizes)
    core = lax.rem(lax.axis_index("exp"), 2)
    pieces, refs = refs[:count], refs[count:]
    if near:
        gate_0, gate_1, pair_0, pair_1 = refs[:4]
        sums, outs = refs[4 : 4 + count], refs[4 + count : 4 + 2 * count]
        rows_x, gate, up, down, sem = refs[4 + 2 * count :]
        up_rows, down_rows = pl.ds(0, FFS), pl.ds(PAIR_DOWN, FFS)
        fetched = (
            ((gate_0, gate_1), gate),
            ((pair_0.at[up_rows], pair_1.at[up_rows]), up),
            ((pair_0.at[down_rows], pair_1.at[down_rows]), down),
        )
    else:
        (gate, up, down), outs = refs[:3], refs[3 : 3 + count]
        rows_x, sem = refs[3 + count :]
        fetched = ()

    def by_core(index, act):
        for which in range(2 if near else 0):

            @pl.when(core == which)
            def _(which=which):
                sources, held = fetched[index]
                act(pltpu.make_async_copy(sources[which], held, sem.at[count + index]))

    copies = []
    start = 0
    for index, (piece, size) in enumerate(zip(pieces, sizes)):
        copies.append(
            pltpu.make_async_copy(piece, rows_x.at[pl.ds(start, size)], sem.at[index])
        )
        start += size
    for copy in copies:
        copy.start()
    for index in range(len(fetched)):
        by_core(index, lambda copy: copy.start())
    for copy in copies:
        copy.wait()
    x = rows_x[...]
    by_core(0, lambda copy: copy.wait())
    g = lax.dot_general(x, gate[...], NT, preferred_element_type=jnp.float32)
    by_core(1, lambda copy: copy.wait())
    v = lax.dot_general(x, up[...], NT, preferred_element_type=jnp.float32)
    act = ((v + 1.0) * g * jax.nn.sigmoid(1.702 * g)).astype(jnp.bfloat16)
    by_core(2, lambda copy: copy.wait())
    for first in range(0, D, 512):
        cols = slice(first, min(first + 512, D))
        part = jnp.dot(act, down[:, cols], preferred_element_type=jnp.float32)
        start = 0
        for index, (out, size) in enumerate(zip(outs, sizes)):
            here = part[start : start + size]
            if near:
                here = here + sums[index][:, cols].astype(jnp.float32)
            out[:, cols] = here.astype(jnp.bfloat16)
            start += size


def experts(pieces, weights, sums=()):
    sizes = tuple(piece.shape[0] for piece in pieces)
    total = sum(sizes)
    near = len(sums) > 0
    return pl.pallas_call(
        functools.partial(expert_kernel, sizes, near),
        out_shape=tuple(jax.ShapeDtypeStruct((size, D), jnp.bfloat16) for size in sizes),
        in_specs=[spec(ANY)] * len(sizes)
        + [spec(ANY if near else VMEM)] * len(weights)
        + [spec(VMEM)] * len(sums),
        out_specs=tuple(spec(VMEM) for _ in sizes),
        scratch_shapes=[pltpu.VMEM((total, D), jnp.bfloat16)]
        + [pltpu.VMEM((FFS, D), jnp.bfloat16)] * (3 if near else 0)
        + [pltpu.SemaphoreType.DMA((len(sizes) + 3,))],
        compiler_params=params(16 if near else 10),
        cost_estimate=pl.CostEstimate(
            flops=6 * total * D * FFS, bytes_accessed=4 << 20, transcendentals=0
        ),
    )(*pieces, *weights, *sums)


def over_all(move):
    pairs = []
    for c in range(8):
        for e in range(16):
            y, x, z, hi, core = move(c // 4, c % 4, e // 4, e // 2 % 2, e % 2)
            pairs.append((c * 16 + e, (y * 4 + x) * 16 + z * 4 + hi * 2 + core))
    return pairs


def partner(y, x, z, hi, core):
    return (1 - y, x, z, hi, core) if core == 0 else (y, x ^ 1, z, hi, core)


def onward(y, x, z, hi, core):
    if core == 0:
        return y, (x + 1) % 4, z, hi, core
    across = x < 2 if y == 0 else x >= 2
    return (y, 3 - x, z, hi, core) if across else (1 - y, x, z, hi, core)


def across_y(y, x, z, hi, core):
    place = (2 * hi + y + (1 if y == 1 else 3)) % 4
    return place % 2, x, z, place // 2, core


def permute(v, pairs):
    return lax.ppermute(v, ("ctx", "exp"), pairs)


NEXT = over_all(onward)
BACK = [(b, a) for a, b in NEXT]
PARTNER = over_all(partner)
PARTNER_0 = [(a, b if a % 2 == 0 else a) for a, b in PARTNER]
PARTNER_1 = [(a, b if a % 2 == 1 else a) for a, b in PARTNER]
ACROSS = over_all(across_y)
SWAP = over_all(lambda y, x, z, hi, core: (y, x, z, hi, 1 - core))


def exchange_experts(arrived, own, near):
    half = TOK // 2
    own_a, own_b = arrived[:half], arrived[half:]
    prev_a, next_b = permute(own_a, NEXT), permute(own_b, BACK)
    prev_b, next_a = permute(own_b, NEXT), permute(own_a, BACK)
    opp_a, opp_b = permute(prev_a, NEXT), permute(next_b, BACK)
    early = (own_a, own_b, prev_a, next_b)
    early_sums = experts(early, own)
    late = (opp_a, opp_b, prev_b, next_a)
    late, early_sums = lax.optimization_barrier((late, early_sums))
    late_sums = experts(late, own)
    near, late_sums = lax.optimization_barrier((near, late_sums))
    far_a, far_b, op_b, on_a = experts(late, near, late_sums)
    far_a, far_b, op_b, on_a, early, early_sums = lax.optimization_barrier(
        (far_a, far_b, op_b, on_a, early, early_sums)
    )
    far_a, far_b = permute(far_a, NEXT), permute(far_b, BACK)
    oo_a, oo_b, op_a, on_b = experts(early, near, early_sums)
    far_a, far_b, oo_a, oo_b, op_a, on_b = lax.optimization_barrier(
        (far_a, far_b, oo_a, oo_b, op_a, on_b)
    )
    from_prev = permute(jnp.stack([add(on_a, far_a), on_b]), NEXT)
    from_next = permute(jnp.stack([op_a, add(op_b, far_b)]), BACK)
    out_a, out_b = add(oo_a, from_prev[0], from_next[0]), add(oo_b, from_prev[1], from_next[1])
    return jnp.concatenate([out_a, out_b], axis=0)


def on_device(
    resid_in,
    queries,
    keys,
    values,
    sinks,
    segments,
    norm_gain,
    out_weight,
    gate_weight,
    up_weight,
    down_weight,
    expert_ids,
    route_weights,
):
    core = lax.axis_index("exp") % 2
    gate, up, down = gate_weight[0].T, up_weight[0].T, down_weight[0]
    w_own = out_weight.T

    mine = lax.dynamic_slice_in_dim(w_own, core * HALF, HALF, 0)
    mine, gate_out = lax.optimization_barrier((mine, gate))
    w_first = permute(mine, ACROSS)
    gate_0 = permute(gate_out, PARTNER_0)

    packed = pack(queries, keys, values, segments)
    packed = lax.all_to_all(
        packed,
        "ctx",
        split_axis=0,
        concat_axis=0,
        tiled=True,
        axis_index_groups=[[0, 1, 2, 3], [4, 5, 6, 7]],
    )
    packed, gate_0, gate_out = lax.optimization_barrier((packed, gate_0, gate))
    low = lax.ppermute(packed[:, :, 1024:], "ctx", [(x, x + 4) for x in range(4)])
    gate_1 = permute(gate_out, PARTNER_1)
    both = pair(up, down)
    low, w_first, both = lax.optimization_barrier((low, w_first, both))
    w_second = permute(w_first, SWAP)
    pair_0 = permute(both, PARTNER_0)

    weights = (w_own, w_first, w_second)
    opp_a, opp_b = project(attend((2,), sinks, packed, low), *weights)
    opp_a, opp_b, packed, low = lax.optimization_barrier((opp_a, opp_b, packed, low))
    from_left, from_right = go_right(opp_a), go_left(opp_b)
    attn = attend((1, 3), sinks, packed, low)
    attn, gate_1 = lax.optimization_barrier((attn, gate_1))
    to_right, to_left = project(attn, *weights, from_left, from_right)
    to_right, to_left, packed, low = lax.optimization_barrier((to_right, to_left, packed, low))
    left, right = go_right(to_right), go_left(to_left)
    own_a, own_b = project(attend((0,), sinks, packed, low), *weights)
    left, right, own_a, own_b, both = lax.optimization_barrier((left, right, own_a, own_b, both))
    pair_1 = permute(both, PARTNER_1)

    ids = expert_ids.T
    hidden, send = norm(
        resid_in.T, own_a, own_b, left, right, norm_gain.reshape(1, D), ids
    )
    arrived = lax.all_to_all(send, "exp", split_axis=0, concat_axis=0, tiled=True)
    arrived, pair_0 = lax.optimization_barrier((arrived, pair_0))
    summed = exchange_experts(arrived, (gate, up, down), (gate_0, gate_1, pair_0, pair_1))
    back = lax.all_to_all(summed, "exp", split_axis=0, concat_axis=0, tiled=True)
    return combine(hidden, back, ids, route_weights.T).T


def solution(mesh):
    placed = (
        P(("exp", "ctx"), None),
        P(("exp", "ctx"), None),
        P(("exp", "ctx"), None),
        P(("exp", "ctx"), None),
        P(),
        P(("exp", "ctx")),
        P(),
        P("ctx", None),
        P("exp", None, "ctx"),
        P("exp", None, "ctx"),
        P("exp", "ctx", None),
        P(("exp", "ctx"), None),
        P(("exp", "ctx"), None),
    )
    return jax.shard_map(
        on_device, mesh=mesh, in_specs=placed, out_specs=P(("exp", "ctx"), None), check_vma=False
    )
```

```python
import functools

import jax
import jax.numpy as jnp
from jax import lax
from jax.experimental import pallas as pl
from jax.experimental.pallas import tpu as pltpu
from jax.sharding import PartitionSpec as P

D = 2880
QUERY_HEADS = 64
KEY_VALUE_HEADS = 8
HEAD_SIZE = 64
ALL_EXPERTS = 128
TOPK = 4
CAP = 8
TOK = 128
FFS = 360
NX = 4
QUARTER = ALL_EXPERTS // TOPK
WINDOW = 4
DOC_ROWS = 16
PACK_ROWS = TOK + DOC_ROWS
PACK_COLS = 1280
HALF = D // 2
MIB = 1024 * 1024

VMEM = pltpu.VMEM
ANY = pl.ANY
SMEM = pltpu.SMEM

RIGHT = [(4 * y + x, 4 * y + (x + 1) % 4) for y in range(2) for x in range(4)]
LEFT = [(4 * y + x, 4 * y + (x + 3) % 4) for y in range(2) for x in range(4)]
FLIP = [(c, c ^ 4) for c in range(8)]

NT = (((1,), (1,)), ((), ()))
TN = (((0,), (0,)), ((), ()))


def go_right(v):
    return lax.ppermute(v, "ctx", RIGHT)


def go_left(v):
    return lax.ppermute(v, "ctx", LEFT)


def go_flip(v):
    return lax.ppermute(v, "ctx", FLIP)


def params(mib):
    return pltpu.CompilerParams(vmem_limit_bytes=mib * MIB)


def spec(space):
    return pl.BlockSpec(memory_space=space)


def add(*pieces):
    total = pieces[0].astype(jnp.float32)
    for piece in pieces[1:]:
        total = total + piece.astype(jnp.float32)
    return total.astype(jnp.bfloat16)


def pack_kernel(q_ref, k_ref, v_ref, seg_ref, out_ref):
    lane = lax.broadcasted_iota(jnp.int32, (TOK, 128), 1)
    docs = jnp.broadcast_to(seg_ref[...].astype(jnp.float32), (DOC_ROWS, 128))
    eighth = jnp.asarray(0.125, jnp.bfloat16)
    for x in range(NX):
        out_ref[x, :TOK, 0:512] = q_ref[:, 512 * x : 512 * x + 512] * eighth
        out_ref[x, :TOK, 512:1024] = q_ref[:, 2048 + 512 * x : 2048 + 512 * x + 512] * eighth
        for ref, start in ((k_ref, 1024), (v_ref, 1152)):
            base = 128 * (x // 2)
            low = ref[:, base : base + 128].astype(jnp.float32)
            high = ref[:, 256 + base : 256 + base + 128].astype(jnp.float32)
            if x % 2 == 0:
                high = pltpu.roll(high, 64, 1)
            else:
                low = pltpu.roll(low, 64, 1)
            out_ref[x, :TOK, start : start + 128] = jnp.where(lane < 64, low, high).astype(
                jnp.bfloat16
            )
        out_ref[x, TOK:, 0:1024] = jnp.zeros((DOC_ROWS, 1024), jnp.bfloat16)
        out_ref[x, TOK:, 1024:1152] = docs.astype(jnp.bfloat16)
        out_ref[x, TOK:, 1152:1280] = jnp.zeros((DOC_ROWS, 128), jnp.bfloat16)


def pack(queries, keys, values, segments):
    return pl.pallas_call(
        pack_kernel,
        out_shape=jax.ShapeDtypeStruct((NX, PACK_ROWS, PACK_COLS), jnp.bfloat16),
        in_specs=[spec(VMEM)] * 4,
        out_specs=spec(VMEM),
        compiler_params=params(10),
        cost_estimate=pl.CostEstimate(flops=0, bytes_accessed=5 << 20, transcendentals=0),
    )(queries, keys, values, segments.reshape(1, TOK))


def attend_kernel(steps, sinks, pack_ref, low_ref, out_ref, key_a, key_b, val_a, val_b, doc_row, bias, hold):
    ctx = lax.axis_index("ctx")
    y, x = ctx // NX, lax.rem(ctx, NX)
    lane = lax.broadcasted_iota(jnp.int32, (TOK, 128), 1)

    def place(ref, b, first, slot):
        rows = pl.ds(pl.multiple_of(slot * TOK, TOK), TOK)
        keys = ref[b, 0:TOK, first : first + 128].astype(jnp.float32)
        vals = ref[b, 0:TOK, first + 128 : first + 256].astype(jnp.float32)
        for g in range(2):
            mine = (lane < 64) if g == 0 else (lane >= 64)
            k_here = jnp.where(mine, keys, 0.0)
            v_here = jnp.where(mine, vals, 1.0)
            k_roll = pltpu.roll(k_here, 64, 1)
            v_roll = pltpu.roll(v_here, 64, 1)
            pair_k = (k_here, k_roll) if g == 0 else (k_roll, k_here)
            pair_v = (v_here, v_roll) if g == 0 else (v_roll, v_here)
            key_a[g, rows] = pair_k[0].astype(jnp.bfloat16)
            key_b[g, rows] = pair_k[1].astype(jnp.bfloat16)
            val_a[g, rows] = pair_v[0].astype(jnp.bfloat16)
            val_b[g, rows] = pair_v[1].astype(jnp.bfloat16)
        doc_row[:, rows] = ref[b, TOK : TOK + 8, first : first + 128].astype(jnp.float32)

    for b in range(NX):
        place(pack_ref, b, 1024, 4 * y + b)

    @pl.when(y == 1)
    def _():
        for b in range(NX):
            place(low_ref, b, 0, b)

    two = 2 * TOK
    upper = lax.broadcasted_iota(jnp.int32, (two, 128), 0) < TOK
    first = lax.broadcasted_iota(jnp.int32, (two, 128), 1) < 64

    def block_rows(index, carry):
        j = lax.rem(x + steps[0] + index * (steps[-1] - steps[0]), NX)
        block = 4 * y + j
        own_docs = doc_row[0:1, pl.ds(pl.multiple_of(block * TOK, TOK), TOK)]
        query_docs = jnp.transpose(jnp.broadcast_to(own_docs, (TOK, TOK)))
        query_place = block * TOK + lax.broadcasted_iota(jnp.int32, (TOK, 128), 0)

        def run(chunks):
            for t in range(2 * chunks):
                cols = slice(128 * t, 128 * t + 128)
                allowed = (query_docs == doc_row[0:1, cols]) & (128 * t + lane <= query_place)
                bias[:, cols] = jnp.where(allowed, 0.0, -jnp.inf)

            def quad(p, carry):
                g = p // 2
                base = pl.multiple_of(p * 256, 256)
                place_out = pl.multiple_of(512 * lax.rem(g + y, 2) + 256 * lax.rem(p, 2), 256)
                q = jnp.concatenate(
                    [
                        pack_ref[j, 0:TOK, pl.ds(base, 128)],
                        pack_ref[j, 0:TOK, pl.ds(pl.multiple_of(base + 128, 128), 128)],
                    ],
                    axis=0,
                )
                head = 8 * x + 32 * g + 4 * lax.rem(p, 2)
                tops, sink_rows = [], []
                for which, key_ref in enumerate((key_a, key_b)):
                    sink = jnp.where(upper, sinks[head + which], sinks[head + 2 + which])
                    top = sink
                    for c in range(chunks):
                        cols = slice(256 * c, 256 * c + 256)
                        s = lax.dot_general(
                            q, key_ref[g, cols], NT, preferred_element_type=jnp.float32
                        )
                        mask = bias[:, cols]
                        s = s + jnp.concatenate([mask, mask], axis=0)
                        hold[which, :, cols] = s
                        top = jnp.maximum(top, jnp.maximum(s[:, 0:128], s[:, 128:256]))
                    tops.append(jnp.max(top, axis=1, keepdims=True))
                    sink_rows.append(sink)
                outs = []
                for which, val_ref in enumerate((val_a, val_b)):
                    total = jnp.zeros((two, 128), jnp.float32)
                    for c in range(chunks):
                        cols = slice(256 * c, 256 * c + 256)
                        prob = jnp.exp(hold[which, :, cols] - tops[which]).astype(jnp.bfloat16)
                        total = total + jnp.dot(
                            prob, val_ref[g, cols], preferred_element_type=jnp.float32
                        )
                    outs.append(total)
                numer = jnp.where(first, outs[0], outs[1])
                divisor = pltpu.roll(jnp.where(first, outs[1], outs[0]), 64, 1)
                gap = jnp.where(first, sink_rows[0] - tops[0], sink_rows[1] - tops[1])
                result = (numer / (divisor + jnp.exp(gap))).astype(jnp.bfloat16)
                rows = pl.ds(pl.multiple_of(index * TOK, TOK), TOK)
                out_ref[rows, pl.ds(place_out, 128)] = result[0:TOK]
                out_ref[rows, pl.ds(pl.multiple_of(place_out + 128, 128), 128)] = result[TOK:]
                return carry

            lax.fori_loop(0, 4, quad, 0)

        for quarter in range(4):

            @pl.when(block // 2 == quarter)
            def _(quarter=quarter):
                run(quarter + 1)

        return carry

    lax.fori_loop(0, len(steps), block_rows, 0)


def attend(steps, sinks, packed, low):
    return pl.pallas_call(
        functools.partial(attend_kernel, steps),
        out_shape=jax.ShapeDtypeStruct((len(steps) * TOK, 1024), jnp.bfloat16),
        in_specs=[spec(SMEM), spec(VMEM), spec(VMEM)],
        out_specs=spec(VMEM),
        scratch_shapes=[
            pltpu.VMEM((2, 1024, 128), jnp.bfloat16),
            pltpu.VMEM((2, 1024, 128), jnp.bfloat16),
            pltpu.VMEM((2, 1024, 128), jnp.bfloat16),
            pltpu.VMEM((2, 1024, 128), jnp.bfloat16),
            pltpu.VMEM((8, 1024), jnp.float32),
            pltpu.VMEM((TOK, 1024), jnp.float32),
            pltpu.VMEM((2, 2 * TOK, 1024), jnp.float32),
        ],
        compiler_params=params(11),
        cost_estimate=pl.CostEstimate(
            flops=2 << 30, bytes_accessed=4 << 20, transcendentals=0
        ),
    )(sinks, packed, low)


def project_kernel(sides, attn, w_own, w_first, w_second, *refs):
    core = lax.rem(lax.axis_index("exp"), 2)
    if sides:
        from_left, from_right, to_right, to_left = refs
    else:
        out_a, out_b = refs
    for part, (w_near, base) in enumerate(((w_first, core * HALF), (w_second, (1 - core) * HALF))):
        for start in range(0, HALF, 288):
            near = slice(start, start + 288)
            rows = pl.ds(pl.multiple_of(base + start, 16), 288)
            total = lax.dot_general(
                w_own[rows], attn[:, 0:512], NT, preferred_element_type=jnp.float32
            ) + lax.dot_general(
                w_near[near], attn[:, 512:1024], NT, preferred_element_type=jnp.float32
            )
            if not sides:
                (out_a, out_b)[part][near] = total.astype(jnp.bfloat16)
                continue
            after, before = total[:, 0:128], total[:, 128:256]
            if part == 0:
                after = after + from_left[near].astype(jnp.float32)
            else:
                before = before + from_right[near].astype(jnp.float32)
            to_right[rows] = after.astype(jnp.bfloat16)
            to_left[rows] = before.astype(jnp.bfloat16)


def project(attn, w_own, w_first, w_second, *extra):
    sides = len(extra) > 0
    rows = D if sides else HALF
    return pl.pallas_call(
        functools.partial(project_kernel, sides),
        out_shape=(jax.ShapeDtypeStruct((rows, TOK), jnp.bfloat16),) * 2,
        in_specs=[spec(VMEM)] * (4 + len(extra)),
        out_specs=(spec(VMEM),) * 2,
        compiler_params=params(10),
        cost_estimate=pl.CostEstimate(flops=3 << 29, bytes_accessed=4 << 20, transcendentals=0),
    )(attn, w_own, w_first, w_second, *extra)


def slot_table(ids):
    local = ids % QUARTER
    chosen = jnp.where(local < WINDOW, ids // QUARTER * WINDOW + local, -1)
    slot = lax.broadcasted_iota(jnp.int32, (TOK, TOK), 0)
    expert = slot // CAP
    hits = [chosen[k : k + 1] == expert for k in range(TOPK)]
    named = functools.reduce(jnp.logical_or, hits)
    before = lax.broadcasted_iota(jnp.int32, (TOK, TOK), 0) < lax.broadcasted_iota(
        jnp.int32, (TOK, TOK), 1
    )
    rank = jnp.dot(
        jnp.where(named, 1.0, 0.0).astype(jnp.bfloat16),
        jnp.where(before, 1.0, 0.0).astype(jnp.bfloat16),
        preferred_element_type=jnp.float32,
    )
    table = named & (rank == (slot % CAP).astype(jnp.float32))
    return table, hits


def norm_kernel(resid, own_a, own_b, left, right, gain, ids, hidden_ref, send_ref, gain_row):
    core = lax.rem(lax.axis_index("exp"), 2)
    gain_row[...] = jnp.ones_like(gain_row)
    gain_row[:, 0:D] = gain[...]
    square = jnp.zeros((8, TOK), jnp.float32)
    for base, own in ((core * HALF, own_a), ((1 - core) * HALF, own_b)):
        for start in range(0, HALF, 160):
            rows = pl.ds(pl.multiple_of(base + start, 16), 160)
            total = own[start : start + 160].astype(jnp.float32)
            total = total + left[rows].astype(jnp.float32) + right[rows].astype(jnp.float32)
            hidden = resid[rows].astype(jnp.float32) + total
            hidden_ref[rows] = hidden
            square = square + jnp.sum((hidden * hidden).reshape(20, 8, TOK), axis=0)
    mean = jnp.sum(square, axis=0, keepdims=True) * (1.0 / D)
    scale = lax.rsqrt(mean + 1e-05)
    table, _ = slot_table(ids[...])
    table = jnp.where(table, 1.0, 0.0).astype(jnp.bfloat16)
    for start in range(0, D, 128):
        size = min(128, D - start)
        rows = slice(start, start + size)
        gains = jnp.transpose(jnp.broadcast_to(gain_row[:, start : start + 128], (128, 128)))
        normed = (hidden_ref[rows] * scale * gains[0:size]).astype(jnp.bfloat16)
        send_ref[:, rows] = lax.dot_general(
            table, normed, NT, preferred_element_type=jnp.float32
        ).astype(jnp.bfloat16)


def norm(resid, own_a, own_b, left, right, gain, ids):
    return pl.pallas_call(
        norm_kernel,
        out_shape=(
            jax.ShapeDtypeStruct((D, TOK), jnp.float32),
            jax.ShapeDtypeStruct((TOK, D), jnp.bfloat16),
        ),
        in_specs=[spec(VMEM)] * 7,
        out_specs=(spec(VMEM), spec(VMEM)),
        scratch_shapes=[pltpu.VMEM((1, D + 64), jnp.float32)],
        compiler_params=params(10),
        cost_estimate=pl.CostEstimate(flops=1 << 27, bytes_accessed=6 << 20, transcendentals=0),
    )(resid, own_a, own_b, left, right, gain, ids)


def combine_kernel(hidden, back, ids, weights, out_ref):
    table, hits = slot_table(ids[...])
    chosen_weight = jnp.zeros((TOK, TOK), jnp.float32)
    for k in range(TOPK):
        chosen_weight = chosen_weight + jnp.where(hits[k], weights[k : k + 1], 0.0)
    share = jnp.where(table, chosen_weight, 0.0)
    high = share.astype(jnp.bfloat16)
    low = (share - high.astype(jnp.float32)).astype(jnp.bfloat16)
    for start in range(0, D, 128):
        cols = slice(start, min(start + 128, D))
        rows = back[:, cols]
        moe = lax.dot_general(rows, high, TN, preferred_element_type=jnp.float32)
        moe = moe + lax.dot_general(rows, low, TN, preferred_element_type=jnp.float32)
        out_ref[cols] = (hidden[cols] + moe).astype(jnp.bfloat16)


def combine(hidden, back, ids, weights):
    return pl.pallas_call(
        combine_kernel,
        out_shape=jax.ShapeDtypeStruct((D, TOK), jnp.bfloat16),
        in_specs=[spec(VMEM)] * 4,
        out_specs=spec(VMEM),
        compiler_params=params(10),
        cost_estimate=pl.CostEstimate(flops=1 << 28, bytes_accessed=3 << 20, transcendentals=0),
    )(hidden, back, ids, weights)


PAIR_DOWN, PAIR_ROWS = 368, 728


def pair_kernel(up, down, out):
    out[0:FFS] = up[...]
    out[FFS:PAIR_DOWN] = jnp.zeros((PAIR_DOWN - FFS, D), jnp.bfloat16)
    out[PAIR_DOWN:PAIR_ROWS] = down[...]


def pair(up, down):
    return pl.pallas_call(
        pair_kernel,
        out_shape=jax.ShapeDtypeStruct((PAIR_ROWS, D), jnp.bfloat16),
        in_specs=[spec(VMEM)] * 2,
        out_specs=spec(VMEM),
        compiler_params=params(10),
        cost_estimate=pl.CostEstimate(flops=0, bytes_accessed=8 << 20, transcendentals=0),
    )(up, down)


def expert_kernel(sizes, near, *refs):
    count = len(sizes)
    core = lax.rem(lax.axis_index("exp"), 2)
    pieces, refs = refs[:count], refs[count:]
    if near:
        gate_0, gate_1, pair_0, pair_1 = refs[:4]
        sums, outs = refs[4 : 4 + count], refs[4 + count : 4 + 2 * count]
        rows_x, gate, up, down, sem = refs[4 + 2 * count :]
        up_rows, down_rows = pl.ds(0, FFS), pl.ds(PAIR_DOWN, FFS)
        fetched = (
            ((gate_0, gate_1), gate),
            ((pair_0.at[up_rows], pair_1.at[up_rows]), up),
            ((pair_0.at[down_rows], pair_1.at[down_rows]), down),
        )
    else:
        (gate, up, down), outs = refs[:3], refs[3 : 3 + count]
        rows_x, sem = refs[3 + count :]
        fetched = ()

    def by_core(index, act):
        for which in range(2 if near else 0):

            @pl.when(core == which)
            def _(which=which):
                sources, held = fetched[index]
                act(pltpu.make_async_copy(sources[which], held, sem.at[count + index]))

    copies = []
    start = 0
    for index, (piece, size) in enumerate(zip(pieces, sizes)):
        copies.append(
            pltpu.make_async_copy(piece, rows_x.at[pl.ds(start, size)], sem.at[index])
        )
        start += size
    for copy in copies:
        copy.start()
    for index in range(len(fetched)):
        by_core(index, lambda copy: copy.start())
    for copy in copies:
        copy.wait()
    x = rows_x[...]
    by_core(0, lambda copy: copy.wait())
    g = lax.dot_general(x, gate[...], NT, preferred_element_type=jnp.float32)
    by_core(1, lambda copy: copy.wait())
    v = lax.dot_general(x, up[...], NT, preferred_element_type=jnp.float32)
    act = ((v + 1.0) * g * jax.nn.sigmoid(1.702 * g)).astype(jnp.bfloat16)
    by_core(2, lambda copy: copy.wait())
    for first in range(0, D, 512):
        cols = slice(first, min(first + 512, D))
        part = jnp.dot(act, down[:, cols], preferred_element_type=jnp.float32)
        start = 0
        for index, (out, size) in enumerate(zip(outs, sizes)):
            here = part[start : start + size]
            if near:
                here = here + sums[index][:, cols].astype(jnp.float32)
            out[:, cols] = here.astype(jnp.bfloat16)
            start += size


def experts(pieces, weights, sums=()):
    sizes = tuple(piece.shape[0] for piece in pieces)
    total = sum(sizes)
    near = len(sums) > 0
    return pl.pallas_call(
        functools.partial(expert_kernel, sizes, near),
        out_shape=tuple(jax.ShapeDtypeStruct((size, D), jnp.bfloat16) for size in sizes),
        in_specs=[spec(ANY)] * len(sizes)
        + [spec(ANY if near else VMEM)] * len(weights)
        + [spec(VMEM)] * len(sums),
        out_specs=tuple(spec(VMEM) for _ in sizes),
        scratch_shapes=[pltpu.VMEM((total, D), jnp.bfloat16)]
        + [pltpu.VMEM((FFS, D), jnp.bfloat16)] * (3 if near else 0)
        + [pltpu.SemaphoreType.DMA((len(sizes) + 3,))],
        compiler_params=params(13 if near else 8),
        cost_estimate=pl.CostEstimate(
            flops=6 * total * D * FFS, bytes_accessed=4 << 20, transcendentals=0
        ),
    )(*pieces, *weights, *sums)


def over_all(move):
    pairs = []
    for c in range(8):
        for e in range(16):
            y, x, z, hi, core = move(c // 4, c % 4, e // 4, e // 2 % 2, e % 2)
            pairs.append((c * 16 + e, (y * 4 + x) * 16 + z * 4 + hi * 2 + core))
    return pairs


def partner(y, x, z, hi, core):
    return (1 - y, x, z, hi, core) if core == 0 else (y, x ^ 1, z, hi, core)


def onward(y, x, z, hi, core):
    if core == 0:
        return y, (x + 1) % 4, z, hi, core
    across = x < 2 if y == 0 else x >= 2
    return (y, 3 - x, z, hi, core) if across else (1 - y, x, z, hi, core)


def across_y(y, x, z, hi, core):
    place = (2 * hi + y + (1 if y == 1 else 3)) % 4
    return place % 2, x, z, place // 2, core


def permute(v, pairs):
    return lax.ppermute(v, ("ctx", "exp"), pairs)


NEXT = over_all(onward)
BACK = [(b, a) for a, b in NEXT]
PARTNER = over_all(partner)
PARTNER_0 = [(a, b) for a, b in PARTNER if a % 2 == 0]
PARTNER_1 = [(a, b) for a, b in PARTNER if a % 2 == 1]
ACROSS = over_all(across_y)
SWAP = over_all(lambda y, x, z, hi, core: (y, x, z, hi, 1 - core))


def odd_place(y, x, z, hi, core):
    return x % 2 == 1 if core == 0 else (x >= 2) == (y == 0)


FORWARD = over_all(lambda *at: onward(*at) if odd_place(*at) else onward(*onward(*onward(*at))))


def exchange_experts(arrived, own, near):
    half = TOK // 2
    y, x = lax.axis_index("ctx") // NX, lax.axis_index("ctx") % NX
    odd = jnp.where(lax.axis_index("exp") % 2 == 0, x % 2 == 1, (x >= 2) == (y == 0))
    own_a, own_b = arrived[:half], arrived[half:]
    prev_a, next_a = permute(own_a, NEXT), permute(own_a, BACK)
    prev_b, next_b = permute(own_b, NEXT), permute(own_b, BACK)
    opp_a = permute(jnp.where(odd, prev_a, next_a), FORWARD)
    opp_b = permute(jnp.where(odd, prev_b, next_b), FORWARD)
    early = (own_a, own_b, prev_a, next_a)
    early_sums = experts(early, own)
    late = (opp_a, opp_b, prev_b, next_b)
    late, early_sums = lax.optimization_barrier((late, early_sums))
    late_sums = experts(late, own)
    near, late_sums = lax.optimization_barrier((near, late_sums))
    far_a, far_b, op_b, on_b = experts(late, near, late_sums)
    far_a, far_b, op_b, on_b, early, early_sums = lax.optimization_barrier(
        (far_a, far_b, op_b, on_b, early, early_sums)
    )
    far_a, far_b = permute(far_a, NEXT), permute(far_b, BACK)
    oo_a, oo_b, op_a, on_a = experts(early, near, early_sums)
    far_a, far_b, oo_a, oo_b, op_a, on_a = lax.optimization_barrier(
        (far_a, far_b, oo_a, oo_b, op_a, on_a)
    )
    from_prev = permute(jnp.stack([add(on_a, far_a), on_b]), NEXT)
    from_next = permute(jnp.stack([op_a, add(op_b, far_b)]), BACK)
    out_a, out_b = add(oo_a, from_prev[0], from_next[0]), add(oo_b, from_prev[1], from_next[1])
    return jnp.concatenate([out_a, out_b], axis=0)


def on_device(
    resid_in,
    queries,
    keys,
    values,
    sinks,
    segments,
    norm_gain,
    out_weight,
    gate_weight,
    up_weight,
    down_weight,
    expert_ids,
    route_weights,
):
    core = lax.axis_index("exp") % 2
    gate, up, down = gate_weight[0].T, up_weight[0].T, down_weight[0]
    w_own = out_weight.T

    mine = lax.dynamic_slice_in_dim(w_own, core * HALF, HALF, 0)
    mine, gate_out = lax.optimization_barrier((mine, gate))
    w_first = permute(mine, ACROSS)
    gate_0 = permute(gate_out, PARTNER_0)

    packed = pack(queries, keys, values, segments)
    packed = lax.all_to_all(
        packed,
        "ctx",
        split_axis=0,
        concat_axis=0,
        tiled=True,
        axis_index_groups=[[0, 1, 2, 3], [4, 5, 6, 7]],
    )
    packed, gate_0, gate_out = lax.optimization_barrier((packed, gate_0, gate))
    low = lax.ppermute(packed[:, :, 1024:], "ctx", [(x, x + 4) for x in range(4)])
    gate_1 = permute(gate_out, PARTNER_1)
    both = pair(up, down)
    low, w_first, both = lax.optimization_barrier((low, w_first, both))
    w_second = permute(w_first, SWAP)
    pair_0 = permute(both, PARTNER_0)

    weights = (w_own, w_first, w_second)
    opp_a, opp_b = project(attend((2,), sinks, packed, low), *weights)
    opp_a, opp_b, packed, low = lax.optimization_barrier((opp_a, opp_b, packed, low))
    from_left, from_right = go_right(opp_a), go_left(opp_b)
    attn = attend((1, 3), sinks, packed, low)
    attn, gate_1 = lax.optimization_barrier((attn, gate_1))
    to_right, to_left = project(attn, *weights, from_left, from_right)
    to_right, to_left, packed, low = lax.optimization_barrier((to_right, to_left, packed, low))
    left, right = go_right(to_right), go_left(to_left)
    own_a, own_b = project(attend((0,), sinks, packed, low), *weights)
    left, right, own_a, own_b, both = lax.optimization_barrier((left, right, own_a, own_b, both))
    pair_1 = permute(both, PARTNER_1)

    ids = expert_ids.T
    hidden, send = norm(
        resid_in.T, own_a, own_b, left, right, norm_gain.reshape(1, D), ids
    )
    arrived = lax.all_to_all(send, "exp", split_axis=0, concat_axis=0, tiled=True)
    arrived, pair_0 = lax.optimization_barrier((arrived, pair_0))
    summed = exchange_experts(arrived, (gate, up, down), (gate_0, gate_1, pair_0, pair_1))
    back = lax.all_to_all(summed, "exp", split_axis=0, concat_axis=0, tiled=True)
    return combine(hidden, back, ids, route_weights.T).T


def solution(mesh):
    placed = (
        P(("exp", "ctx"), None),
        P(("exp", "ctx"), None),
        P(("exp", "ctx"), None),
        P(("exp", "ctx"), None),
        P(),
        P(("exp", "ctx")),
        P(),
        P("ctx", None),
        P("exp", None, "ctx"),
        P("exp", None, "ctx"),
        P("exp", "ctx", None),
        P(("exp", "ctx"), None),
        P(("exp", "ctx"), None),
    )
    return jax.shard_map(
        on_device, mesh=mesh, in_specs=placed, out_specs=P(("exp", "ctx"), None), check_vma=False
    )
```

```python
import functools

import jax
import jax.numpy as jnp
from jax import lax
from jax.experimental import pallas as pl
from jax.experimental.pallas import tpu as pltpu
from jax.sharding import PartitionSpec as P

D = 2880
QUERY_HEADS = 64
KEY_VALUE_HEADS = 8
HEAD_SIZE = 64
ALL_EXPERTS = 128
TOPK = 4
CAP = 8
TOK = 128
FFS = 360
NX = 4
QUARTER = ALL_EXPERTS // TOPK
WINDOW = 4
DOC_ROWS = 16
PACK_ROWS = TOK + DOC_ROWS
PACK_COLS = 1280
HALF = D // 2
MIB = 1024 * 1024

VMEM = pltpu.VMEM
ANY = pl.ANY
SMEM = pltpu.SMEM

RIGHT = [(4 * y + x, 4 * y + (x + 1) % 4) for y in range(2) for x in range(4)]
LEFT = [(4 * y + x, 4 * y + (x + 3) % 4) for y in range(2) for x in range(4)]
FLIP = [(c, c ^ 4) for c in range(8)]

NT = (((1,), (1,)), ((), ()))
TN = (((0,), (0,)), ((), ()))


def go_right(v):
    return lax.ppermute(v, "ctx", RIGHT)


def go_left(v):
    return lax.ppermute(v, "ctx", LEFT)


def go_flip(v):
    return lax.ppermute(v, "ctx", FLIP)


def params(mib):
    return pltpu.CompilerParams(vmem_limit_bytes=mib * MIB)


def spec(space):
    return pl.BlockSpec(memory_space=space)


def add(*pieces):
    total = pieces[0].astype(jnp.float32)
    for piece in pieces[1:]:
        total = total + piece.astype(jnp.float32)
    return total.astype(jnp.bfloat16)


def pack_kernel(q_ref, k_ref, v_ref, seg_ref, out_ref):
    lane = lax.broadcasted_iota(jnp.int32, (TOK, 128), 1)
    docs = jnp.broadcast_to(seg_ref[...].astype(jnp.float32), (DOC_ROWS, 128))
    eighth = jnp.asarray(0.125, jnp.bfloat16)
    for x in range(NX):
        out_ref[x, :TOK, 0:512] = q_ref[:, 512 * x : 512 * x + 512] * eighth
        out_ref[x, :TOK, 512:1024] = q_ref[:, 2048 + 512 * x : 2048 + 512 * x + 512] * eighth
        for ref, start in ((k_ref, 1024), (v_ref, 1152)):
            base = 128 * (x // 2)
            low = ref[:, base : base + 128].astype(jnp.float32)
            high = ref[:, 256 + base : 256 + base + 128].astype(jnp.float32)
            if x % 2 == 0:
                high = pltpu.roll(high, 64, 1)
            else:
                low = pltpu.roll(low, 64, 1)
            out_ref[x, :TOK, start : start + 128] = jnp.where(lane < 64, low, high).astype(
                jnp.bfloat16
            )
        out_ref[x, TOK:, 0:1024] = jnp.zeros((DOC_ROWS, 1024), jnp.bfloat16)
        out_ref[x, TOK:, 1024:1152] = docs.astype(jnp.bfloat16)
        out_ref[x, TOK:, 1152:1280] = jnp.zeros((DOC_ROWS, 128), jnp.bfloat16)


def pack(queries, keys, values, segments):
    return pl.pallas_call(
        pack_kernel,
        out_shape=jax.ShapeDtypeStruct((NX, PACK_ROWS, PACK_COLS), jnp.bfloat16),
        in_specs=[spec(VMEM)] * 4,
        out_specs=spec(VMEM),
        compiler_params=params(10),
        cost_estimate=pl.CostEstimate(flops=0, bytes_accessed=5 << 20, transcendentals=0),
    )(queries, keys, values, segments.reshape(1, TOK))


def attend_kernel(steps, sinks, pack_ref, low_ref, out_ref, key_a, key_b, val_a, val_b, doc_row, bias, hold):
    ctx = lax.axis_index("ctx")
    y, x = ctx // NX, lax.rem(ctx, NX)
    lane = lax.broadcasted_iota(jnp.int32, (TOK, 128), 1)

    def place(ref, b, first, slot):
        rows = pl.ds(pl.multiple_of(slot * TOK, TOK), TOK)
        keys = ref[b, 0:TOK, first : first + 128].astype(jnp.float32)
        vals = ref[b, 0:TOK, first + 128 : first + 256].astype(jnp.float32)
        for g in range(2):
            mine = (lane < 64) if g == 0 else (lane >= 64)
            k_here = jnp.where(mine, keys, 0.0)
            v_here = jnp.where(mine, vals, 1.0)
            k_roll = pltpu.roll(k_here, 64, 1)
            v_roll = pltpu.roll(v_here, 64, 1)
            pair_k = (k_here, k_roll) if g == 0 else (k_roll, k_here)
            pair_v = (v_here, v_roll) if g == 0 else (v_roll, v_here)
            key_a[g, rows] = pair_k[0].astype(jnp.bfloat16)
            key_b[g, rows] = pair_k[1].astype(jnp.bfloat16)
            val_a[g, rows] = pair_v[0].astype(jnp.bfloat16)
            val_b[g, rows] = pair_v[1].astype(jnp.bfloat16)
        doc_row[:, rows] = ref[b, TOK : TOK + 8, first : first + 128].astype(jnp.float32)

    for b in range(NX):
        place(pack_ref, b, 1024, 4 * y + b)

    @pl.when(y == 1)
    def _():
        for b in range(NX):
            place(low_ref, b, 0, b)

    two = 2 * TOK
    upper = lax.broadcasted_iota(jnp.int32, (two, 128), 0) < TOK
    first = lax.broadcasted_iota(jnp.int32, (two, 128), 1) < 64

    def block_rows(index, carry):
        j = lax.rem(x + steps[0] + index * (steps[-1] - steps[0]), NX)
        block = 4 * y + j
        own_docs = doc_row[0:1, pl.ds(pl.multiple_of(block * TOK, TOK), TOK)]
        query_docs = jnp.transpose(jnp.broadcast_to(own_docs, (TOK, TOK)))
        query_place = block * TOK + lax.broadcasted_iota(jnp.int32, (TOK, 128), 0)

        def run(chunks):
            for t in range(2 * chunks):
                cols = slice(128 * t, 128 * t + 128)
                allowed = (query_docs == doc_row[0:1, cols]) & (128 * t + lane <= query_place)
                bias[:, cols] = jnp.where(allowed, 0.0, -jnp.inf)

            def quad(p, carry):
                g = p // 2
                base = pl.multiple_of(p * 256, 256)
                place_out = pl.multiple_of(512 * lax.rem(g + y, 2) + 256 * lax.rem(p, 2), 256)
                q = jnp.concatenate(
                    [
                        pack_ref[j, 0:TOK, pl.ds(base, 128)],
                        pack_ref[j, 0:TOK, pl.ds(pl.multiple_of(base + 128, 128), 128)],
                    ],
                    axis=0,
                )
                head = 8 * x + 32 * g + 4 * lax.rem(p, 2)
                tops, sink_rows = [], []
                for which, key_ref in enumerate((key_a, key_b)):
                    sink = jnp.where(upper, sinks[head + which], sinks[head + 2 + which])
                    top = sink
                    for c in range(chunks):
                        cols = slice(256 * c, 256 * c + 256)
                        s = lax.dot_general(
                            q, key_ref[g, cols], NT, preferred_element_type=jnp.float32
                        )
                        mask = bias[:, cols]
                        s = s + jnp.concatenate([mask, mask], axis=0)
                        hold[which, :, cols] = s
                        top = jnp.maximum(top, jnp.maximum(s[:, 0:128], s[:, 128:256]))
                    tops.append(jnp.max(top, axis=1, keepdims=True))
                    sink_rows.append(sink)
                outs = []
                for which, val_ref in enumerate((val_a, val_b)):
                    total = jnp.zeros((two, 128), jnp.float32)
                    for c in range(chunks):
                        cols = slice(256 * c, 256 * c + 256)
                        prob = jnp.exp(hold[which, :, cols] - tops[which]).astype(jnp.bfloat16)
                        total = total + jnp.dot(
                            prob, val_ref[g, cols], preferred_element_type=jnp.float32
                        )
                    outs.append(total)
                numer = jnp.where(first, outs[0], outs[1])
                divisor = pltpu.roll(jnp.where(first, outs[1], outs[0]), 64, 1)
                gap = jnp.where(first, sink_rows[0] - tops[0], sink_rows[1] - tops[1])
                result = (numer / (divisor + jnp.exp(gap))).astype(jnp.bfloat16)
                rows = pl.ds(pl.multiple_of(index * TOK, TOK), TOK)
                out_ref[rows, pl.ds(place_out, 128)] = result[0:TOK]
                out_ref[rows, pl.ds(pl.multiple_of(place_out + 128, 128), 128)] = result[TOK:]
                return carry

            lax.fori_loop(0, 4, quad, 0)

        for quarter in range(4):

            @pl.when(block // 2 == quarter)
            def _(quarter=quarter):
                run(quarter + 1)

        return carry

    lax.fori_loop(0, len(steps), block_rows, 0)


def attend(steps, sinks, packed, low):
    return pl.pallas_call(
        functools.partial(attend_kernel, steps),
        out_shape=jax.ShapeDtypeStruct((len(steps) * TOK, 1024), jnp.bfloat16),
        in_specs=[spec(SMEM), spec(VMEM), spec(VMEM)],
        out_specs=spec(VMEM),
        scratch_shapes=[
            pltpu.VMEM((2, 1024, 128), jnp.bfloat16),
            pltpu.VMEM((2, 1024, 128), jnp.bfloat16),
            pltpu.VMEM((2, 1024, 128), jnp.bfloat16),
            pltpu.VMEM((2, 1024, 128), jnp.bfloat16),
            pltpu.VMEM((8, 1024), jnp.float32),
            pltpu.VMEM((TOK, 1024), jnp.float32),
            pltpu.VMEM((2, 2 * TOK, 1024), jnp.float32),
        ],
        compiler_params=params(14),
        cost_estimate=pl.CostEstimate(
            flops=2 << 30, bytes_accessed=4 << 20, transcendentals=0
        ),
    )(sinks, packed, low)


def project_kernel(sides, attn, w_own, w_first, w_second, *refs):
    core = lax.rem(lax.axis_index("exp"), 2)
    if sides:
        from_left, from_right, to_right, to_left = refs
    else:
        out_a, out_b = refs
    for part, (w_near, base) in enumerate(((w_first, core * HALF), (w_second, (1 - core) * HALF))):
        for start in range(0, HALF, 288):
            near = slice(start, start + 288)
            rows = pl.ds(pl.multiple_of(base + start, 16), 288)
            total = lax.dot_general(
                w_own[rows], attn[:, 0:512], NT, preferred_element_type=jnp.float32
            ) + lax.dot_general(
                w_near[near], attn[:, 512:1024], NT, preferred_element_type=jnp.float32
            )
            if not sides:
                (out_a, out_b)[part][near] = total.astype(jnp.bfloat16)
                continue
            after, before = total[:, 0:128], total[:, 128:256]
            if part == 0:
                after = after + from_left[near].astype(jnp.float32)
            else:
                before = before + from_right[near].astype(jnp.float32)
            to_right[rows] = after.astype(jnp.bfloat16)
            to_left[rows] = before.astype(jnp.bfloat16)


def project(attn, w_own, w_first, w_second, *extra):
    sides = len(extra) > 0
    rows = D if sides else HALF
    return pl.pallas_call(
        functools.partial(project_kernel, sides),
        out_shape=(jax.ShapeDtypeStruct((rows, TOK), jnp.bfloat16),) * 2,
        in_specs=[spec(VMEM)] * (4 + len(extra)),
        out_specs=(spec(VMEM),) * 2,
        compiler_params=params(10),
        cost_estimate=pl.CostEstimate(flops=3 << 29, bytes_accessed=4 << 20, transcendentals=0),
    )(attn, w_own, w_first, w_second, *extra)


def slot_table(ids):
    local = ids % QUARTER
    chosen = jnp.where(local < WINDOW, ids // QUARTER * WINDOW + local, -1)
    slot = lax.broadcasted_iota(jnp.int32, (TOK, TOK), 0)
    expert = slot // CAP
    hits = [chosen[k : k + 1] == expert for k in range(TOPK)]
    named = functools.reduce(jnp.logical_or, hits)
    before = lax.broadcasted_iota(jnp.int32, (TOK, TOK), 0) < lax.broadcasted_iota(
        jnp.int32, (TOK, TOK), 1
    )
    rank = jnp.dot(
        jnp.where(named, 1.0, 0.0).astype(jnp.bfloat16),
        jnp.where(before, 1.0, 0.0).astype(jnp.bfloat16),
        preferred_element_type=jnp.float32,
    )
    table = named & (rank == (slot % CAP).astype(jnp.float32))
    return table, hits


def norm_kernel(resid, own_a, own_b, left, right, gain, ids, hidden_ref, send_ref, gain_row):
    core = lax.rem(lax.axis_index("exp"), 2)
    gain_row[...] = jnp.ones_like(gain_row)
    gain_row[:, 0:D] = gain[...]
    square = jnp.zeros((8, TOK), jnp.float32)
    for base, own in ((core * HALF, own_a), ((1 - core) * HALF, own_b)):
        for start in range(0, HALF, 160):
            rows = pl.ds(pl.multiple_of(base + start, 16), 160)
            total = own[start : start + 160].astype(jnp.float32)
            total = total + left[rows].astype(jnp.float32) + right[rows].astype(jnp.float32)
            hidden = resid[rows].astype(jnp.float32) + total
            hidden_ref[rows] = hidden
            square = square + jnp.sum((hidden * hidden).reshape(20, 8, TOK), axis=0)
    mean = jnp.sum(square, axis=0, keepdims=True) * (1.0 / D)
    scale = lax.rsqrt(mean + 1e-05)
    table, _ = slot_table(ids[...])
    table = jnp.where(table, 1.0, 0.0).astype(jnp.bfloat16)
    for start in range(0, D, 128):
        size = min(128, D - start)
        rows = slice(start, start + size)
        gains = jnp.transpose(jnp.broadcast_to(gain_row[:, start : start + 128], (128, 128)))
        normed = (hidden_ref[rows] * scale * gains[0:size]).astype(jnp.bfloat16)
        send_ref[:, rows] = lax.dot_general(
            table, normed, NT, preferred_element_type=jnp.float32
        ).astype(jnp.bfloat16)


def norm(resid, own_a, own_b, left, right, gain, ids):
    return pl.pallas_call(
        norm_kernel,
        out_shape=(
            jax.ShapeDtypeStruct((D, TOK), jnp.float32),
            jax.ShapeDtypeStruct((TOK, D), jnp.bfloat16),
        ),
        in_specs=[spec(VMEM)] * 7,
        out_specs=(spec(VMEM), spec(VMEM)),
        scratch_shapes=[pltpu.VMEM((1, D + 64), jnp.float32)],
        compiler_params=params(10),
        cost_estimate=pl.CostEstimate(flops=1 << 27, bytes_accessed=6 << 20, transcendentals=0),
    )(resid, own_a, own_b, left, right, gain, ids)


def combine_kernel(hidden, back, ids, weights, out_ref):
    table, hits = slot_table(ids[...])
    chosen_weight = jnp.zeros((TOK, TOK), jnp.float32)
    for k in range(TOPK):
        chosen_weight = chosen_weight + jnp.where(hits[k], weights[k : k + 1], 0.0)
    share = jnp.where(table, chosen_weight, 0.0)
    high = share.astype(jnp.bfloat16)
    low = (share - high.astype(jnp.float32)).astype(jnp.bfloat16)
    for start in range(0, D, 128):
        cols = slice(start, min(start + 128, D))
        rows = back[:, cols]
        moe = lax.dot_general(rows, high, TN, preferred_element_type=jnp.float32)
        moe = moe + lax.dot_general(rows, low, TN, preferred_element_type=jnp.float32)
        out_ref[cols] = (hidden[cols] + moe).astype(jnp.bfloat16)


def combine(hidden, back, ids, weights):
    return pl.pallas_call(
        combine_kernel,
        out_shape=jax.ShapeDtypeStruct((D, TOK), jnp.bfloat16),
        in_specs=[spec(VMEM)] * 4,
        out_specs=spec(VMEM),
        compiler_params=params(10),
        cost_estimate=pl.CostEstimate(flops=1 << 28, bytes_accessed=3 << 20, transcendentals=0),
    )(hidden, back, ids, weights)


PAIR_DOWN, PAIR_ROWS = 368, 728


def pair_kernel(up, down, out):
    out[0:FFS] = up[...]
    out[FFS:PAIR_DOWN] = jnp.zeros((PAIR_DOWN - FFS, D), jnp.bfloat16)
    out[PAIR_DOWN:PAIR_ROWS] = down[...]


def pair(up, down):
    return pl.pallas_call(
        pair_kernel,
        out_shape=jax.ShapeDtypeStruct((PAIR_ROWS, D), jnp.bfloat16),
        in_specs=[spec(VMEM)] * 2,
        out_specs=spec(VMEM),
        compiler_params=params(10),
        cost_estimate=pl.CostEstimate(flops=0, bytes_accessed=8 << 20, transcendentals=0),
    )(up, down)


def expert_kernel(sizes, near, *refs):
    count = len(sizes)
    core = lax.rem(lax.axis_index("exp"), 2)
    pieces, refs = refs[:count], refs[count:]
    if near:
        gate_0, gate_1, pair_0, pair_1 = refs[:4]
        sums, outs = refs[4 : 4 + count], refs[4 + count : 4 + 2 * count]
        rows_x, gate, up, down, sem = refs[4 + 2 * count :]
        up_rows, down_rows = pl.ds(0, FFS), pl.ds(PAIR_DOWN, FFS)
        fetched = (
            ((gate_0, gate_1), gate),
            ((pair_0.at[up_rows], pair_1.at[up_rows]), up),
            ((pair_0.at[down_rows], pair_1.at[down_rows]), down),
        )
    else:
        (gate, up, down), outs = refs[:3], refs[3 : 3 + count]
        rows_x, sem = refs[3 + count :]
        fetched = ()

    def by_core(index, act):
        for which in range(2 if near else 0):

            @pl.when(core == which)
            def _(which=which):
                sources, held = fetched[index]
                act(pltpu.make_async_copy(sources[which], held, sem.at[count + index]))

    copies = []
    start = 0
    for index, (piece, size) in enumerate(zip(pieces, sizes)):
        copies.append(
            pltpu.make_async_copy(piece, rows_x.at[pl.ds(start, size)], sem.at[index])
        )
        start += size
    for copy in copies:
        copy.start()
    for index in range(len(fetched)):
        by_core(index, lambda copy: copy.start())
    for copy in copies:
        copy.wait()
    x = rows_x[...]
    by_core(0, lambda copy: copy.wait())
    g = lax.dot_general(x, gate[...], NT, preferred_element_type=jnp.float32)
    by_core(1, lambda copy: copy.wait())
    v = lax.dot_general(x, up[...], NT, preferred_element_type=jnp.float32)
    act = ((v + 1.0) * g * jax.nn.sigmoid(1.702 * g)).astype(jnp.bfloat16)
    by_core(2, lambda copy: copy.wait())
    for first in range(0, D, 512):
        cols = slice(first, min(first + 512, D))
        part = jnp.dot(act, down[:, cols], preferred_element_type=jnp.float32)
        start = 0
        for index, (out, size) in enumerate(zip(outs, sizes)):
            here = part[start : start + size]
            if near:
                here = here + sums[index][:, cols].astype(jnp.float32)
            out[:, cols] = here.astype(jnp.bfloat16)
            start += size


def experts(pieces, weights, sums=()):
    sizes = tuple(piece.shape[0] for piece in pieces)
    total = sum(sizes)
    near = len(sums) > 0
    return pl.pallas_call(
        functools.partial(expert_kernel, sizes, near),
        out_shape=tuple(jax.ShapeDtypeStruct((size, D), jnp.bfloat16) for size in sizes),
        in_specs=[spec(ANY)] * len(sizes)
        + [spec(ANY if near else VMEM)] * len(weights)
        + [spec(VMEM)] * len(sums),
        out_specs=tuple(spec(VMEM) for _ in sizes),
        scratch_shapes=[pltpu.VMEM((total, D), jnp.bfloat16)]
        + [pltpu.VMEM((FFS, D), jnp.bfloat16)] * (3 if near else 0)
        + [pltpu.SemaphoreType.DMA((len(sizes) + 3,))],
        compiler_params=params(16),
        cost_estimate=pl.CostEstimate(
            flops=6 * total * D * FFS, bytes_accessed=4 << 20, transcendentals=0
        ),
    )(*pieces, *weights, *sums)


def over_all(move):
    pairs = []
    for c in range(8):
        for e in range(16):
            y, x, z, hi, core = move(c // 4, c % 4, e // 4, e // 2 % 2, e % 2)
            pairs.append((c * 16 + e, (y * 4 + x) * 16 + z * 4 + hi * 2 + core))
    return pairs


def partner(y, x, z, hi, core):
    return (1 - y, x, z, hi, core) if core == 0 else (y, x ^ 1, z, hi, core)


def onward(y, x, z, hi, core):
    if core == 0:
        return y, (x + 1) % 4, z, hi, core
    across = x < 2 if y == 0 else x >= 2
    return (y, 3 - x, z, hi, core) if across else (1 - y, x, z, hi, core)


def across_y(y, x, z, hi, core):
    place = (2 * hi + y + (1 if y == 1 else 3)) % 4
    return place % 2, x, z, place // 2, core


def permute(v, pairs):
    return lax.ppermute(v, ("ctx", "exp"), pairs)


NEXT = over_all(onward)
BACK = [(b, a) for a, b in NEXT]
PARTNER = over_all(partner)
PARTNER_0 = [(a, b) for a, b in PARTNER if a % 2 == 0]
PARTNER_1 = [(a, b) for a, b in PARTNER if a % 2 == 1]
ACROSS = over_all(across_y)
SWAP = over_all(lambda y, x, z, hi, core: (y, x, z, hi, 1 - core))


def exchange_experts(arrived, own, near):
    half = TOK // 2
    own_a, own_b = arrived[:half], arrived[half:]
    prev_a, next_b = permute(own_a, NEXT), permute(own_b, BACK)
    prev_b, next_a = permute(own_b, NEXT), permute(own_a, BACK)
    opp_a, opp_b = permute(prev_a, NEXT), permute(next_b, BACK)
    early = (own_a, own_b, prev_a, next_b)
    early_sums = experts(early, own)
    late = (opp_a, opp_b, prev_b, next_a)
    late, early_sums = lax.optimization_barrier((late, early_sums))
    late_sums = experts(late, own)
    near, late_sums = lax.optimization_barrier((near, late_sums))
    far_a, far_b = experts(late[:2], near, late_sums[:2])
    far_a, far_b, early, early_sums = lax.optimization_barrier((far_a, far_b, early, early_sums))
    far_a, far_b = permute(far_a, NEXT), permute(far_b, BACK)
    oo_a, oo_b, op_a, on_b, op_b, on_a = experts(
        early + late[2:], near, early_sums + late_sums[2:]
    )
    far_a, far_b, oo_a, oo_b, op_a, on_b, op_b, on_a = lax.optimization_barrier(
        (far_a, far_b, oo_a, oo_b, op_a, on_b, op_b, on_a)
    )
    from_prev = permute(jnp.stack([add(on_a, far_a), on_b]), NEXT)
    from_next = permute(jnp.stack([op_a, add(op_b, far_b)]), BACK)
    out_a, out_b = add(oo_a, from_prev[0], from_next[0]), add(oo_b, from_prev[1], from_next[1])
    return jnp.concatenate([out_a, out_b], axis=0)


def on_device(
    resid_in,
    queries,
    keys,
    values,
    sinks,
    segments,
    norm_gain,
    out_weight,
    gate_weight,
    up_weight,
    down_weight,
    expert_ids,
    route_weights,
):
    core = lax.axis_index("exp") % 2
    gate, up, down = gate_weight[0].T, up_weight[0].T, down_weight[0]
    w_own = out_weight.T

    mine = lax.dynamic_slice_in_dim(w_own, core * HALF, HALF, 0)
    mine, gate_out = lax.optimization_barrier((mine, gate))
    w_first = permute(mine, ACROSS)
    gate_0 = permute(gate_out, PARTNER_0)

    packed = pack(queries, keys, values, segments)
    packed = lax.all_to_all(
        packed,
        "ctx",
        split_axis=0,
        concat_axis=0,
        tiled=True,
        axis_index_groups=[[0, 1, 2, 3], [4, 5, 6, 7]],
    )
    packed, gate_0, gate_out = lax.optimization_barrier((packed, gate_0, gate))
    low = lax.ppermute(packed[:, :, 1024:], "ctx", [(x, x + 4) for x in range(4)])
    gate_1 = permute(gate_out, PARTNER_1)
    both = pair(up, down)
    low, w_first, both = lax.optimization_barrier((low, w_first, both))
    w_second = permute(w_first, SWAP)
    pair_0 = permute(both, PARTNER_0)

    weights = (w_own, w_first, w_second)
    opp_a, opp_b = project(attend((2,), sinks, packed, low), *weights)
    opp_a, opp_b, packed, low = lax.optimization_barrier((opp_a, opp_b, packed, low))
    from_left, from_right = go_right(opp_a), go_left(opp_b)
    attn = attend((1, 3), sinks, packed, low)
    attn, gate_1 = lax.optimization_barrier((attn, gate_1))
    to_right, to_left = project(attn, *weights, from_left, from_right)
    to_right, to_left, packed, low = lax.optimization_barrier((to_right, to_left, packed, low))
    left, right = go_right(to_right), go_left(to_left)
    own_a, own_b = project(attend((0,), sinks, packed, low), *weights)
    left, right, own_a, own_b, both = lax.optimization_barrier((left, right, own_a, own_b, both))
    pair_1 = permute(both, PARTNER_1)

    ids = expert_ids.T
    hidden, send = norm(
        resid_in.T, own_a, own_b, left, right, norm_gain.reshape(1, D), ids
    )
    arrived = lax.all_to_all(send, "exp", split_axis=0, concat_axis=0, tiled=True)
    arrived, pair_0 = lax.optimization_barrier((arrived, pair_0))
    summed = exchange_experts(arrived, (gate, up, down), (gate_0, gate_1, pair_0, pair_1))
    back = lax.all_to_all(summed, "exp", split_axis=0, concat_axis=0, tiled=True)
    return combine(hidden, back, ids, route_weights.T).T


def solution(mesh):
    placed = (
        P(("exp", "ctx"), None),
        P(("exp", "ctx"), None),
        P(("exp", "ctx"), None),
        P(("exp", "ctx"), None),
        P(),
        P(("exp", "ctx")),
        P(),
        P("ctx", None),
        P("exp", None, "ctx"),
        P("exp", None, "ctx"),
        P("exp", "ctx", None),
        P(("exp", "ctx"), None),
        P(("exp", "ctx"), None),
    )
    return jax.shard_map(
        on_device, mesh=mesh, in_specs=placed, out_specs=P(("exp", "ctx"), None), check_vma=False
    )
```

```python
import functools

import jax
import jax.numpy as jnp
from jax import lax
from jax.experimental import pallas as pl
from jax.experimental.pallas import tpu as pltpu
from jax.sharding import PartitionSpec as P

D = 2880
QUERY_HEADS = 64
KEY_VALUE_HEADS = 8
HEAD_SIZE = 64
ALL_EXPERTS = 128
TOPK = 4
CAP = 8
TOK = 128
FFS = 360
NX = 4
QUARTER = ALL_EXPERTS // TOPK
WINDOW = 4
DOC_ROWS = 8
PACK_ROWS = TOK + DOC_ROWS
PACK_COLS = 1280
HALF = D // 2
MIB = 1024 * 1024

VMEM = pltpu.VMEM
ANY = pl.ANY
SMEM = pltpu.SMEM

RIGHT = [(4 * y + x, 4 * y + (x + 1) % 4) for y in range(2) for x in range(4)]
LEFT = [(4 * y + x, 4 * y + (x + 3) % 4) for y in range(2) for x in range(4)]
FLIP = [(c, c ^ 4) for c in range(8)]

NT = (((1,), (1,)), ((), ()))
TN = (((0,), (0,)), ((), ()))


def go_right(v):
    return lax.ppermute(v, "ctx", RIGHT)


def go_left(v):
    return lax.ppermute(v, "ctx", LEFT)


def go_flip(v):
    return lax.ppermute(v, "ctx", FLIP)


def params(mib):
    return pltpu.CompilerParams(vmem_limit_bytes=mib * MIB)


def spec(space):
    return pl.BlockSpec(memory_space=space)


def add(*pieces):
    total = pieces[0].astype(jnp.float32)
    for piece in pieces[1:]:
        total = total + piece.astype(jnp.float32)
    return total.astype(jnp.bfloat16)


def pack_kernel(q_ref, k_ref, v_ref, seg_ref, out_ref):
    lane = lax.broadcasted_iota(jnp.int32, (TOK, 128), 1)
    docs = jnp.broadcast_to(seg_ref[...].astype(jnp.float32), (DOC_ROWS, 128))
    eighth = jnp.asarray(0.125, jnp.bfloat16)
    for x in range(NX):
        out_ref[x, :TOK, 0:512] = q_ref[:, 512 * x : 512 * x + 512] * eighth
        out_ref[x, :TOK, 512:1024] = q_ref[:, 2048 + 512 * x : 2048 + 512 * x + 512] * eighth
        for ref, start in ((k_ref, 1024), (v_ref, 1152)):
            base = 128 * (x // 2)
            low = ref[:, base : base + 128].astype(jnp.float32)
            high = ref[:, 256 + base : 256 + base + 128].astype(jnp.float32)
            if x % 2 == 0:
                high = pltpu.roll(high, 64, 1)
            else:
                low = pltpu.roll(low, 64, 1)
            out_ref[x, :TOK, start : start + 128] = jnp.where(lane < 64, low, high).astype(
                jnp.bfloat16
            )
        out_ref[x, TOK:, 0:1024] = jnp.zeros((DOC_ROWS, 1024), jnp.bfloat16)
        out_ref[x, TOK:, 1024:1152] = docs.astype(jnp.bfloat16)
        out_ref[x, TOK:, 1152:1280] = jnp.zeros((DOC_ROWS, 128), jnp.bfloat16)


def pack(queries, keys, values, segments):
    return pl.pallas_call(
        pack_kernel,
        out_shape=jax.ShapeDtypeStruct((NX, PACK_ROWS, PACK_COLS), jnp.bfloat16),
        in_specs=[spec(VMEM)] * 4,
        out_specs=spec(VMEM),
        compiler_params=params(10),
        cost_estimate=pl.CostEstimate(flops=0, bytes_accessed=5 << 20, transcendentals=0),
    )(queries, keys, values, segments.reshape(1, TOK))


def attend_kernel(steps, sinks, pack_ref, low_ref, out_ref, key_a, key_b, val_a, val_b, doc_row, bias, hold):
    ctx = lax.axis_index("ctx")
    y, x = ctx // NX, lax.rem(ctx, NX)
    lane = lax.broadcasted_iota(jnp.int32, (TOK, 128), 1)

    def place(ref, b, first, slot):
        rows = pl.ds(pl.multiple_of(slot * TOK, TOK), TOK)
        keys = ref[b, 0:TOK, first : first + 128].astype(jnp.float32)
        vals = ref[b, 0:TOK, first + 128 : first + 256].astype(jnp.float32)
        for g in range(2):
            mine = (lane < 64) if g == 0 else (lane >= 64)
            k_here = jnp.where(mine, keys, 0.0)
            v_here = jnp.where(mine, vals, 1.0)
            k_roll = pltpu.roll(k_here, 64, 1)
            v_roll = pltpu.roll(v_here, 64, 1)
            pair_k = (k_here, k_roll) if g == 0 else (k_roll, k_here)
            pair_v = (v_here, v_roll) if g == 0 else (v_roll, v_here)
            key_a[g, rows] = pair_k[0].astype(jnp.bfloat16)
            key_b[g, rows] = pair_k[1].astype(jnp.bfloat16)
            val_a[g, rows] = pair_v[0].astype(jnp.bfloat16)
            val_b[g, rows] = pair_v[1].astype(jnp.bfloat16)
        doc_row[:, rows] = ref[b, TOK : TOK + 8, first : first + 128].astype(jnp.float32)

    for b in range(NX):
        place(pack_ref, b, 1024, 4 * y + b)

    @pl.when(y == 1)
    def _():
        for b in range(NX):
            place(low_ref, b, 0, b)

    two = 2 * TOK
    upper = lax.broadcasted_iota(jnp.int32, (two, 128), 0) < TOK
    first = lax.broadcasted_iota(jnp.int32, (two, 128), 1) < 64

    def block_rows(index, carry):
        j = lax.rem(x + steps[0] + index * (steps[-1] - steps[0]), NX)
        block = 4 * y + j
        own_docs = doc_row[0:1, pl.ds(pl.multiple_of(block * TOK, TOK), TOK)]
        query_docs = jnp.transpose(jnp.broadcast_to(own_docs, (TOK, TOK)))
        query_place = block * TOK + lax.broadcasted_iota(jnp.int32, (TOK, 128), 0)

        def run(chunks):
            for t in range(2 * chunks):
                cols = slice(128 * t, 128 * t + 128)
                allowed = (query_docs == doc_row[0:1, cols]) & (128 * t + lane <= query_place)
                bias[:, cols] = jnp.where(allowed, 0.0, -jnp.inf)

            def quad(p, carry):
                g = p // 2
                base = pl.multiple_of(p * 256, 256)
                place_out = pl.multiple_of(512 * lax.rem(g + y, 2) + 256 * lax.rem(p, 2), 256)
                q = jnp.concatenate(
                    [
                        pack_ref[j, 0:TOK, pl.ds(base, 128)],
                        pack_ref[j, 0:TOK, pl.ds(pl.multiple_of(base + 128, 128), 128)],
                    ],
                    axis=0,
                )
                head = 8 * x + 32 * g + 4 * lax.rem(p, 2)
                tops, sink_rows = [], []
                for which, key_ref in enumerate((key_a, key_b)):
                    sink = jnp.where(upper, sinks[head + which], sinks[head + 2 + which])
                    top = sink
                    for c in range(chunks):
                        cols = slice(256 * c, 256 * c + 256)
                        s = lax.dot_general(
                            q, key_ref[g, cols], NT, preferred_element_type=jnp.float32
                        )
                        mask = bias[:, cols]
                        s = s + jnp.concatenate([mask, mask], axis=0)
                        hold[which, :, cols] = s
                        top = jnp.maximum(top, jnp.maximum(s[:, 0:128], s[:, 128:256]))
                    tops.append(jnp.max(top, axis=1, keepdims=True))
                    sink_rows.append(sink)
                outs = []
                for which, val_ref in enumerate((val_a, val_b)):
                    total = jnp.zeros((two, 128), jnp.float32)
                    for c in range(chunks):
                        cols = slice(256 * c, 256 * c + 256)
                        prob = jnp.exp(hold[which, :, cols] - tops[which]).astype(jnp.bfloat16)
                        total = total + jnp.dot(
                            prob, val_ref[g, cols], preferred_element_type=jnp.float32
                        )
                    outs.append(total)
                numer = jnp.where(first, outs[0], outs[1])
                divisor = pltpu.roll(jnp.where(first, outs[1], outs[0]), 64, 1)
                gap = jnp.where(first, sink_rows[0] - tops[0], sink_rows[1] - tops[1])
                result = (numer / (divisor + jnp.exp(gap))).astype(jnp.bfloat16)
                rows = pl.ds(pl.multiple_of(index * TOK, TOK), TOK)
                out_ref[rows, pl.ds(place_out, 128)] = result[0:TOK]
                out_ref[rows, pl.ds(pl.multiple_of(place_out + 128, 128), 128)] = result[TOK:]
                return carry

            lax.fori_loop(0, 4, quad, 0)

        for quarter in range(4):

            @pl.when(block // 2 == quarter)
            def _(quarter=quarter):
                run(quarter + 1)

        return carry

    lax.fori_loop(0, len(steps), block_rows, 0)


def attend(steps, sinks, packed, low):
    return pl.pallas_call(
        functools.partial(attend_kernel, steps),
        out_shape=jax.ShapeDtypeStruct((len(steps) * TOK, 1024), jnp.bfloat16),
        in_specs=[spec(SMEM), spec(VMEM), spec(VMEM)],
        out_specs=spec(VMEM),
        scratch_shapes=[
            pltpu.VMEM((2, 1024, 128), jnp.bfloat16),
            pltpu.VMEM((2, 1024, 128), jnp.bfloat16),
            pltpu.VMEM((2, 1024, 128), jnp.bfloat16),
            pltpu.VMEM((2, 1024, 128), jnp.bfloat16),
            pltpu.VMEM((8, 1024), jnp.float32),
            pltpu.VMEM((TOK, 1024), jnp.float32),
            pltpu.VMEM((2, 2 * TOK, 1024), jnp.float32),
        ],
        compiler_params=params(14),
        cost_estimate=pl.CostEstimate(
            flops=2 << 30, bytes_accessed=4 << 20, transcendentals=0
        ),
    )(sinks, packed, low)


def project_kernel(sides, attn, w_own, w_first, w_second, *refs):
    core = lax.rem(lax.axis_index("exp"), 2)
    if sides:
        from_left, from_right, to_right, to_left = refs
    else:
        out_a, out_b = refs
    for part, (w_near, base) in enumerate(((w_first, core * HALF), (w_second, (1 - core) * HALF))):
        for start in range(0, HALF, 288):
            near = slice(start, start + 288)
            rows = pl.ds(pl.multiple_of(base + start, 16), 288)
            total = lax.dot_general(
                w_own[rows], attn[:, 0:512], NT, preferred_element_type=jnp.float32
            ) + lax.dot_general(
                w_near[near], attn[:, 512:1024], NT, preferred_element_type=jnp.float32
            )
            if not sides:
                (out_a, out_b)[part][near] = total.astype(jnp.bfloat16)
                continue
            after, before = total[:, 0:128], total[:, 128:256]
            if part == 0:
                after = after + from_left[near].astype(jnp.float32)
            else:
                before = before + from_right[near].astype(jnp.float32)
            to_right[rows] = after.astype(jnp.bfloat16)
            to_left[rows] = before.astype(jnp.bfloat16)


def project(attn, w_own, w_first, w_second, *extra):
    sides = len(extra) > 0
    rows = D if sides else HALF
    return pl.pallas_call(
        functools.partial(project_kernel, sides),
        out_shape=(jax.ShapeDtypeStruct((rows, TOK), jnp.bfloat16),) * 2,
        in_specs=[spec(VMEM)] * (4 + len(extra)),
        out_specs=(spec(VMEM),) * 2,
        compiler_params=params(10),
        cost_estimate=pl.CostEstimate(flops=3 << 29, bytes_accessed=4 << 20, transcendentals=0),
    )(attn, w_own, w_first, w_second, *extra)


def slot_table(ids):
    local = ids % QUARTER
    chosen = jnp.where(local < WINDOW, ids // QUARTER * WINDOW + local, -1)
    slot = lax.broadcasted_iota(jnp.int32, (TOK, TOK), 0)
    expert = slot // CAP
    hits = [chosen[k : k + 1] == expert for k in range(TOPK)]
    named = functools.reduce(jnp.logical_or, hits)
    before = lax.broadcasted_iota(jnp.int32, (TOK, TOK), 0) < lax.broadcasted_iota(
        jnp.int32, (TOK, TOK), 1
    )
    rank = jnp.dot(
        jnp.where(named, 1.0, 0.0).astype(jnp.bfloat16),
        jnp.where(before, 1.0, 0.0).astype(jnp.bfloat16),
        preferred_element_type=jnp.float32,
    )
    table = named & (rank == (slot % CAP).astype(jnp.float32))
    return table, hits


def norm_kernel(resid, own_a, own_b, left, right, gain, ids, hidden_ref, send_ref, gain_row):
    core = lax.rem(lax.axis_index("exp"), 2)
    gain_row[...] = jnp.ones_like(gain_row)
    gain_row[:, 0:D] = gain[...]
    square = jnp.zeros((8, TOK), jnp.float32)
    for base, own in ((core * HALF, own_a), ((1 - core) * HALF, own_b)):
        for start in range(0, HALF, 160):
            rows = pl.ds(pl.multiple_of(base + start, 16), 160)
            total = own[start : start + 160].astype(jnp.float32)
            total = total + left[rows].astype(jnp.float32) + right[rows].astype(jnp.float32)
            hidden = resid[rows].astype(jnp.float32) + total
            hidden_ref[rows] = hidden
            square = square + jnp.sum((hidden * hidden).reshape(20, 8, TOK), axis=0)
    mean = jnp.sum(square, axis=0, keepdims=True) * (1.0 / D)
    scale = lax.rsqrt(mean + 1e-05)
    table, _ = slot_table(ids[...])
    table = jnp.where(table, 1.0, 0.0).astype(jnp.bfloat16)
    for start in range(0, D, 128):
        size = min(128, D - start)
        rows = slice(start, start + size)
        gains = jnp.transpose(jnp.broadcast_to(gain_row[:, start : start + 128], (128, 128)))
        normed = (hidden_ref[rows] * scale * gains[0:size]).astype(jnp.bfloat16)
        send_ref[:, rows] = lax.dot_general(
            table, normed, NT, preferred_element_type=jnp.float32
        ).astype(jnp.bfloat16)


def norm(resid, own_a, own_b, left, right, gain, ids):
    return pl.pallas_call(
        norm_kernel,
        out_shape=(
            jax.ShapeDtypeStruct((D, TOK), jnp.float32),
            jax.ShapeDtypeStruct((TOK, D), jnp.bfloat16),
        ),
        in_specs=[spec(VMEM)] * 7,
        out_specs=(spec(VMEM), spec(VMEM)),
        scratch_shapes=[pltpu.VMEM((1, D + 64), jnp.float32)],
        compiler_params=params(10),
        cost_estimate=pl.CostEstimate(flops=1 << 27, bytes_accessed=6 << 20, transcendentals=0),
    )(resid, own_a, own_b, left, right, gain, ids)


def combine_kernel(hidden, back, ids, weights, out_ref):
    table, hits = slot_table(ids[...])
    chosen_weight = jnp.zeros((TOK, TOK), jnp.float32)
    for k in range(TOPK):
        chosen_weight = chosen_weight + jnp.where(hits[k], weights[k : k + 1], 0.0)
    share = jnp.where(table, chosen_weight, 0.0)
    high = share.astype(jnp.bfloat16)
    low = (share - high.astype(jnp.float32)).astype(jnp.bfloat16)
    for start in range(0, D, 128):
        cols = slice(start, min(start + 128, D))
        rows = back[:, cols]
        moe = lax.dot_general(rows, high, TN, preferred_element_type=jnp.float32)
        moe = moe + lax.dot_general(rows, low, TN, preferred_element_type=jnp.float32)
        out_ref[cols] = (hidden[cols] + moe).astype(jnp.bfloat16)


def combine(hidden, back, ids, weights):
    return pl.pallas_call(
        combine_kernel,
        out_shape=jax.ShapeDtypeStruct((D, TOK), jnp.bfloat16),
        in_specs=[spec(VMEM)] * 4,
        out_specs=spec(VMEM),
        compiler_params=params(10),
        cost_estimate=pl.CostEstimate(flops=1 << 28, bytes_accessed=3 << 20, transcendentals=0),
    )(hidden, back, ids, weights)


PAIR_DOWN, PAIR_ROWS = 368, 728


def pair_kernel(up, down, out):
    out[0:FFS] = up[...]
    out[FFS:PAIR_DOWN] = jnp.zeros((PAIR_DOWN - FFS, D), jnp.bfloat16)
    out[PAIR_DOWN:PAIR_ROWS] = down[...]


def pair(up, down):
    return pl.pallas_call(
        pair_kernel,
        out_shape=jax.ShapeDtypeStruct((PAIR_ROWS, D), jnp.bfloat16),
        in_specs=[spec(VMEM)] * 2,
        out_specs=spec(VMEM),
        compiler_params=params(10),
        cost_estimate=pl.CostEstimate(flops=0, bytes_accessed=8 << 20, transcendentals=0),
    )(up, down)


def expert_kernel(sizes, near, *refs):
    count = len(sizes)
    core = lax.rem(lax.axis_index("exp"), 2)
    pieces, refs = refs[:count], refs[count:]
    if near:
        gate_0, gate_1, pair_0, pair_1 = refs[:4]
        sums, outs = refs[4 : 4 + count], refs[4 + count : 4 + 2 * count]
        rows_x, gate, up, down, sem = refs[4 + 2 * count :]
        up_rows, down_rows = pl.ds(0, FFS), pl.ds(PAIR_DOWN, FFS)
        fetched = (
            ((gate_0, gate_1), gate),
            ((pair_0.at[up_rows], pair_1.at[up_rows]), up),
            ((pair_0.at[down_rows], pair_1.at[down_rows]), down),
        )
    else:
        (gate, up, down), outs = refs[:3], refs[3 : 3 + count]
        rows_x, sem = refs[3 + count :]
        fetched = ()

    def by_core(index, act):
        for which in range(2 if near else 0):

            @pl.when(core == which)
            def _(which=which):
                sources, held = fetched[index]
                act(pltpu.make_async_copy(sources[which], held, sem.at[count + index]))

    copies = []
    start = 0
    for index, (piece, size) in enumerate(zip(pieces, sizes)):
        copies.append(
            pltpu.make_async_copy(piece, rows_x.at[pl.ds(start, size)], sem.at[index])
        )
        start += size
    for copy in copies:
        copy.start()
    for index in range(len(fetched)):
        by_core(index, lambda copy: copy.start())
    for copy in copies:
        copy.wait()
    x = rows_x[...]
    by_core(0, lambda copy: copy.wait())
    g = lax.dot_general(x, gate[...], NT, preferred_element_type=jnp.float32)
    by_core(1, lambda copy: copy.wait())
    v = lax.dot_general(x, up[...], NT, preferred_element_type=jnp.float32)
    act = ((v + 1.0) * g * jax.nn.sigmoid(1.702 * g)).astype(jnp.bfloat16)
    by_core(2, lambda copy: copy.wait())
    for first in range(0, D, 512):
        cols = slice(first, min(first + 512, D))
        part = jnp.dot(act, down[:, cols], preferred_element_type=jnp.float32)
        start = 0
        for index, (out, size) in enumerate(zip(outs, sizes)):
            here = part[start : start + size]
            if near:
                here = here + sums[index][:, cols].astype(jnp.float32)
            out[:, cols] = here.astype(jnp.bfloat16)
            start += size


def experts(pieces, weights, sums=()):
    sizes = tuple(piece.shape[0] for piece in pieces)
    total = sum(sizes)
    near = len(sums) > 0
    return pl.pallas_call(
        functools.partial(expert_kernel, sizes, near),
        out_shape=tuple(jax.ShapeDtypeStruct((size, D), jnp.bfloat16) for size in sizes),
        in_specs=[spec(ANY)] * len(sizes)
        + [spec(ANY if near else VMEM)] * len(weights)
        + [spec(VMEM)] * len(sums),
        out_specs=tuple(spec(VMEM) for _ in sizes),
        scratch_shapes=[pltpu.VMEM((total, D), jnp.bfloat16)]
        + [pltpu.VMEM((FFS, D), jnp.bfloat16)] * (3 if near else 0)
        + [pltpu.SemaphoreType.DMA((len(sizes) + 3,))],
        compiler_params=params(16),
        cost_estimate=pl.CostEstimate(
            flops=6 * total * D * FFS, bytes_accessed=4 << 20, transcendentals=0
        ),
    )(*pieces, *weights, *sums)


def over_all(move):
    pairs = []
    for c in range(8):
        for e in range(16):
            y, x, z, hi, core = move(c // 4, c % 4, e // 4, e // 2 % 2, e % 2)
            pairs.append((c * 16 + e, (y * 4 + x) * 16 + z * 4 + hi * 2 + core))
    return pairs


def partner(y, x, z, hi, core):
    return (1 - y, x, z, hi, core) if core == 0 else (y, x ^ 1, z, hi, core)


def onward(y, x, z, hi, core):
    if core == 0:
        return y, (x + 1) % 4, z, hi, core
    across = x < 2 if y == 0 else x >= 2
    return (y, 3 - x, z, hi, core) if across else (1 - y, x, z, hi, core)


def across_y(y, x, z, hi, core):
    place = (2 * hi + y + (1 if y == 1 else 3)) % 4
    return place % 2, x, z, place // 2, core


def permute(v, pairs):
    return lax.ppermute(v, ("ctx", "exp"), pairs)


NEXT = over_all(onward)
BACK = [(b, a) for a, b in NEXT]
PARTNER = over_all(partner)
PARTNER_0 = [(a, b) for a, b in PARTNER if a % 2 == 0]
PARTNER_1 = [(a, b) for a, b in PARTNER if a % 2 == 1]
ACROSS = over_all(across_y)
SWAP = over_all(lambda y, x, z, hi, core: (y, x, z, hi, 1 - core))


def exchange_experts(arrived, own, near):
    half = TOK // 2
    own_a, own_b = arrived[:half], arrived[half:]
    prev_a, next_b = permute(own_a, NEXT), permute(own_b, BACK)
    prev_b, next_a = permute(own_b, NEXT), permute(own_a, BACK)
    opp_a, opp_b = permute(prev_a, NEXT), permute(next_b, BACK)
    early = (own_a, own_b, prev_a, next_b)
    early_sums = experts(early, own)
    late = (opp_a, opp_b, prev_b, next_a)
    late, early_sums = lax.optimization_barrier((late, early_sums))
    late_sums = experts(late, own)
    near, late_sums = lax.optimization_barrier((near, late_sums))
    far_a, far_b = experts(late[:2], near, late_sums[:2])
    far_a, far_b, early, early_sums = lax.optimization_barrier((far_a, far_b, early, early_sums))
    far_a, far_b = permute(far_a, NEXT), permute(far_b, BACK)
    oo_a, oo_b, op_a, on_b, op_b, on_a = experts(
        early + late[2:], near, early_sums + late_sums[2:]
    )
    far_a, far_b, oo_a, oo_b, op_a, on_b, op_b, on_a = lax.optimization_barrier(
        (far_a, far_b, oo_a, oo_b, op_a, on_b, op_b, on_a)
    )
    from_prev = permute(jnp.stack([add(on_a, far_a), on_b]), NEXT)
    from_next = permute(jnp.stack([op_a, add(op_b, far_b)]), BACK)
    out_a, out_b = add(oo_a, from_prev[0], from_next[0]), add(oo_b, from_prev[1], from_next[1])
    return jnp.concatenate([out_a, out_b], axis=0)


def on_device(
    resid_in,
    queries,
    keys,
    values,
    sinks,
    segments,
    norm_gain,
    out_weight,
    gate_weight,
    up_weight,
    down_weight,
    expert_ids,
    route_weights,
):
    core = lax.axis_index("exp") % 2
    gate, up, down = gate_weight[0].T, up_weight[0].T, down_weight[0]
    w_own = out_weight.T

    mine = lax.dynamic_slice_in_dim(w_own, core * HALF, HALF, 0)
    mine, gate_out = lax.optimization_barrier((mine, gate))
    w_first = permute(mine, ACROSS)
    gate_0 = permute(gate_out, PARTNER_0)

    packed = pack(queries, keys, values, segments)
    packed = lax.all_to_all(
        packed,
        "ctx",
        split_axis=0,
        concat_axis=0,
        tiled=True,
        axis_index_groups=[[0, 1, 2, 3], [4, 5, 6, 7]],
    )
    packed, gate_0, gate_out = lax.optimization_barrier((packed, gate_0, gate))
    low = lax.ppermute(packed[:, :, 1024:], "ctx", [(x, x + 4) for x in range(4)])
    gate_1 = permute(gate_out, PARTNER_1)
    both = pair(up, down)
    low, w_first, both = lax.optimization_barrier((low, w_first, both))
    w_second = permute(w_first, SWAP)
    pair_0 = permute(both, PARTNER_0)

    weights = (w_own, w_first, w_second)
    opp_a, opp_b = project(attend((2,), sinks, packed, low), *weights)
    opp_a, opp_b, packed, low = lax.optimization_barrier((opp_a, opp_b, packed, low))
    from_left, from_right = go_right(opp_a), go_left(opp_b)
    attn = attend((1, 3), sinks, packed, low)
    attn, gate_1 = lax.optimization_barrier((attn, gate_1))
    to_right, to_left = project(attn, *weights, from_left, from_right)
    to_right, to_left, packed, low = lax.optimization_barrier((to_right, to_left, packed, low))
    left, right = go_right(to_right), go_left(to_left)
    own_a, own_b = project(attend((0,), sinks, packed, low), *weights)
    left, right, own_a, own_b, both = lax.optimization_barrier((left, right, own_a, own_b, both))
    pair_1 = permute(both, PARTNER_1)

    ids = expert_ids.T
    hidden, send = norm(
        resid_in.T, own_a, own_b, left, right, norm_gain.reshape(1, D), ids
    )
    arrived = lax.all_to_all(send, "exp", split_axis=0, concat_axis=0, tiled=True)
    arrived, pair_0 = lax.optimization_barrier((arrived, pair_0))
    summed = exchange_experts(arrived, (gate, up, down), (gate_0, gate_1, pair_0, pair_1))
    back = lax.all_to_all(summed, "exp", split_axis=0, concat_axis=0, tiled=True)
    return combine(hidden, back, ids, route_weights.T).T


def solution(mesh):
    placed = (
        P(("exp", "ctx"), None),
        P(("exp", "ctx"), None),
        P(("exp", "ctx"), None),
        P(("exp", "ctx"), None),
        P(),
        P(("exp", "ctx")),
        P(),
        P("ctx", None),
        P("exp", None, "ctx"),
        P("exp", None, "ctx"),
        P("exp", "ctx", None),
        P(("exp", "ctx"), None),
        P(("exp", "ctx"), None),
    )
    return jax.shard_map(
        on_device, mesh=mesh, in_specs=placed, out_specs=P(("exp", "ctx"), None), check_vma=False
    )
```
